256 devices in a mesh: atom: 64 (over y, z, core), col: 4 (over x).
Axes of the slice: x: 4, y: 4, z: 8, core: 2. Of those that a mesh axis runs over, the one named last changes fastest.
Arguments:
- atom_single: bfloat16 [32768, 128], P('atom'), may hold values from -6 to 6
- positions: float32 [3, 32768], P(None, 'atom'), may hold values from -96 to 96
- noise_index: int32 [1], replicated, may hold values from 0 to 199
- token_counts: int32 [2048], P('atom'), may hold values from 1 to 256, as said below
- token_single: bfloat16 [2048, 768], P('atom'), may hold values from -6 to 6
- pair_repr: bfloat16 [2048, 2048, 128], P('atom', 'col')
- w_pos: float32 [3, 128], replicated, may hold values from -3.5 to 3.5
- atom_wq: bfloat16 [128, 128], replicated
- atom_wk: bfloat16 [128, 128], replicated
- atom_wv: bfloat16 [128, 128], replicated, may hold values from -0.5 to 0.5
- atom_wo: bfloat16 [128, 128], replicated, may hold values from -0.5 to 0.5
- w_pool: bfloat16 [128, 768], replicated, may hold values from -0.5 to 0.5
- trans_w1: bfloat16 [128, 512], replicated, may hold values from -0.5 to 0.5
- trans_w2: bfloat16 [256, 128], replicated, may hold values from -0.375 to 0.375
- w_bias: bfloat16 [128, 16], replicated, may hold values from -1.5 to 1.5
- token_wq: bfloat16 [768, 768], P(None, 'col')
- token_wk: bfloat16 [768, 768], P(None, 'col')
- token_wv: bfloat16 [768, 768], P(None, 'col'), may hold values from -0.21875 to 0.21875
- token_wo: bfloat16 [768, 768], P('col'), may hold values from -0.21875 to 0.21875
- w_back: bfloat16 [768, 128], replicated, may hold values from -0.21875 to 0.21875
Outputs:
- atom_out: bfloat16 [32768, 128], P('atom')
- pair_out: bfloat16 [2048, 2048, 128], P('atom', 'col')
The draws below stay inside these ranges and needn't reach their ends.
Inputs may be any that keep to these rules, and one draw needn't show every extreme that they name: `token_counts`: tokens form aligned runs of 32; the counts of one run sum to at most 512, and to exactly 512 in at least one run; some token has exactly 256 atoms.
All inputs are finite; a program needn't handle non-finite values.
Results may differ from the reference program's by a relative error of at most 0.018.
Values may be sent and summed in bfloat16 or wider, within the bound.
No kernel may reach another device: no remote copies, remote signals or barrier semaphores. Data moves between devices by JAX's collectives and lax.ppermute only.
A program may use at most 64 MiB of HBM per device.

```python
import math
import jax
import jax.numpy as jnp
from jax import lax

C_A = 128
H_A = 4
C_Z = 128
HID_Z = 256
C_S = 768
H_T = 16
WIN_Q = 32
WIN_K = 128
STEPS = 200
TOK_DEV = 32
ATOM_DEV = 512
NTOK = 2048
NATOM = 32768


def shared_projection(key, salt, rows, columns):
    return jax.random.normal(jax.random.fold_in(key, salt), (rows, columns), jnp.float32) * rows ** (-0.5)


def draw_atom_wq(key, part):
    return shared_projection(key, 101, C_A, C_A).astype(jnp.bfloat16)


def draw_atom_wk(key, part):
    key = jax.random.fold_in(key, 2)
    fresh_key = jax.random.fold_in(key, 0)
    fresh = jax.random.normal(fresh_key, (C_A, C_A), jnp.float32) * C_A ** (-0.5)
    return fresh.astype(jnp.bfloat16)


def draw_token_wq(key, part):
    return shared_projection(key, 202, C_S, C_S).astype(jnp.bfloat16)


def draw_token_wk(key, part):
    key = jax.random.fold_in(key, 3)
    fresh_key = jax.random.fold_in(key, 0)
    fresh = jax.random.normal(fresh_key, (C_S, C_S), jnp.float32) * C_S ** (-0.5)
    return fresh.astype(jnp.bfloat16)


def draw_pair_repr(key, part):
    key = jax.random.fold_in(key, 5)
    noise_key, cell_key, chan_key = jax.random.split(key, 3)
    cell_scale = jnp.exp(jax.random.uniform(cell_key, (NTOK, NTOK, 1), jnp.float32, math.log(0.3), math.log(3.0)))
    chan_scale = jnp.exp(jax.random.uniform(chan_key, (C_Z,), jnp.float32, math.log(0.3), math.log(3.0)))
    noise = jax.random.normal(noise_key, (NTOK, NTOK, C_Z), jnp.float32)
    return (cell_scale * chan_scale * noise).astype(jnp.bfloat16)


def split_counts(extra, weights):
    shares = extra[:, None] * weights // jnp.sum(weights, axis=1, keepdims=True)
    remainder = extra - jnp.sum(shares, axis=1)
    width = weights.shape[1]
    shares = shares + (jnp.arange(width)[None, :] < remainder[:, None]).astype(jnp.int32)
    return 1 + shares


def draw_token_counts(key, part):
    key = jax.random.fold_in(key, 11)
    total_key, full_key, weight_key, rest_key = jax.random.split(key, 4)
    run_count = NTOK // TOK_DEV
    most = 8 * TOK_DEV
    totals = jax.random.randint(total_key, (run_count,), ATOM_DEV // 3, ATOM_DEV + 1)
    weights = jax.random.randint(weight_key, (run_count, TOK_DEV), 1, 9)
    counts = jnp.minimum(split_counts(totals - TOK_DEV, weights), most)
    rest_weights = jax.random.randint(rest_key, (1, TOK_DEV - 1), 1, 9)
    rest_extra = jnp.full((1,), ATOM_DEV - most - (TOK_DEV - 1), jnp.int32)
    rest = split_counts(rest_extra, rest_weights)
    full_row = jnp.concatenate([jnp.full((1, 1), most, jnp.int32), rest], axis=1)
    full_run = jax.random.randint(full_key, (), 0, run_count)
    counts = jnp.where((jnp.arange(run_count) == full_run)[:, None], full_row, counts)
    return counts.reshape(-1).astype(jnp.int32)


def steps_of(rng, dims, shards, least, largest):
    def one(position, shards_of):
        draws = jax.random.uniform(jax.random.fold_in(jax.random.fold_in(rng, 6), position), (shards_of,), jnp.float32, least / len(shards), largest / len(shards))
        return jnp.repeat(jnp.exp(draws), dims[position] // shards_of).reshape((-1,) + (1,) * (len(dims) - position - 1))

    gain = one(*shards[0])
    for cut in shards[1:]:
        gain = gain * one(*cut)
    return gain


def normal_values(key, extent, scale, reach, pieces=(), held_as=jnp.bfloat16):
    result = jax.random.normal(key, extent, jnp.float32) * scale
    if len(pieces) > 0:
        result = steps_of(key, extent, pieces, -0.22, 0.18) * result
    return jnp.clip(result, min=-reach, max=reach).astype(held_as)


def setup_inputs(seed: int = 0) -> dict:
    splits = jax.random.split(jax.random.key(seed), 21)
    return {
        "atom_single": normal_values(splits[0], (NATOM, C_A), 1.0, 6.0, ((0, 64),)),
        "positions": normal_values(splits[1], (3, NATOM), 16.0, 96.0, ((1, 64),), jnp.float32),
        "noise_index": jax.random.randint(splits[2], (1,), 0, STEPS).astype(jnp.int32),
        "token_counts": draw_token_counts(jax.random.fold_in(splits[20], 71), 0),
        "token_single": normal_values(splits[4], (NTOK, C_S), 1.0, 6.0, ((0, 64),)),
        "pair_repr": draw_pair_repr(jax.random.fold_in(splits[20], 71), 0),
        "w_pos": normal_values(splits[6], (3, C_A), 3 ** -0.5, 3.5, (), jnp.float32),
        "atom_wq": draw_atom_wq(jax.random.fold_in(splits[20], 71), 0),
        "atom_wk": draw_atom_wk(jax.random.fold_in(splits[20], 71), 0),
        "atom_wv": normal_values(splits[9], (C_A, C_A), C_A ** -0.5, 0.5),
        "atom_wo": normal_values(splits[10], (C_A, C_A), C_A ** -0.5, 0.5),
        "w_pool": normal_values(splits[11], (C_A, C_S), C_A ** -0.5, 0.5),
        "trans_w1": normal_values(splits[12], (C_Z, 2 * HID_Z), C_Z ** -0.5, 0.5),
        "trans_w2": normal_values(splits[13], (HID_Z, C_Z), HID_Z ** -0.5, 0.375),
        "w_bias": normal_values(splits[14], (C_Z, H_T), (C_Z // 9) ** -0.5, 1.5),
        "token_wq": draw_token_wq(jax.random.fold_in(splits[20], 71), 0),
        "token_wk": draw_token_wk(jax.random.fold_in(splits[20], 71), 0),
        "token_wv": normal_values(splits[17], (C_S, C_S), C_S ** -0.5, 0.21875, ((1, 4),)),
        "token_wo": normal_values(splits[18], (C_S, C_S), C_S ** -0.5, 0.21875, ((0, 4),)),
        "w_back": normal_values(splits[19], (C_S, C_A), C_S ** -0.5, 0.21875),
    }


EPS = 1e-05
SIGMA_DATA = 16.0
SIGMA_MAX = 160.0
SIGMA_MIN = 0.0004
RHO = 7.0
MASKED = -1000000000.0

def normalize(values):
    average = lax.optimization_barrier(jnp.mean(values, axis=-1, keepdims=True))
    centred = values - average
    variance = lax.optimization_barrier(jnp.mean(centred * centred, axis=-1, keepdims=True))
    return centred * lax.rsqrt(variance + EPS)

def noise_scale(noise_index):
    level = noise_index[0].astype(jnp.float32)
    upper = SIGMA_MAX ** (1.0 / RHO)
    lower = SIGMA_MIN ** (1.0 / RHO)
    sigma_now = (upper + level / (STEPS - 1) * (lower - upper)) ** RHO
    return 1.0 / jnp.sqrt(sigma_now * sigma_now + SIGMA_DATA * SIGMA_DATA)

def pair_block(pair_rows, trans_w1, trans_w2, w_bias):
    row_count, col_count, channels = pair_rows.shape
    flattened = pair_rows.reshape(row_count * col_count, channels).astype(jnp.float32)
    normed_in = normalize(flattened).astype(jnp.bfloat16)
    gate_up = jnp.dot(normed_in, trans_w1, preferred_element_type=jnp.float32)
    half_width = gate_up.shape[1] // 2
    hidden = (jax.nn.silu(gate_up[:, :half_width]) * gate_up[:, half_width:]).astype(jnp.bfloat16)
    updated = flattened + jnp.dot(hidden, trans_w2, preferred_element_type=jnp.float32)
    normed_out = normalize(updated).astype(jnp.bfloat16)
    head_bias = lax.dot_general(w_bias, normed_out, (((0,), (1,)), ((), ())), preferred_element_type=jnp.float32)
    head_bias = head_bias.astype(jnp.bfloat16).reshape(-1, row_count, col_count)
    return (updated.astype(jnp.bfloat16).reshape(row_count, col_count, channels), head_bias)

def window_attention(queries, padded_kv, padded_live, head_count):
    length, feat_width = queries.shape
    windows = length // WIN_Q
    key_blocks = WIN_K // WIN_Q
    head_size = feat_width // head_count
    blocks = padded_kv.reshape(windows + key_blocks - 1, WIN_Q, 2 * feat_width)
    key_marks = padded_live.reshape(windows + key_blocks - 1, WIN_Q)
    key_rows = jnp.concatenate([blocks[offset:offset + windows] for offset in range(key_blocks)], axis=1)
    alive_keys = jnp.concatenate([key_marks[offset:offset + windows] for offset in range(key_blocks)], axis=1)
    query_part = queries.reshape(windows, WIN_Q, head_count, head_size).astype(jnp.float32)
    key_part = key_rows[:, :, :feat_width].reshape(windows, WIN_K, head_count, head_size).astype(jnp.float32)
    value_part = key_rows[:, :, feat_width:].reshape(windows, WIN_K, head_count, head_size).astype(jnp.float32)
    scores = jnp.einsum('wqhd,wkhd->whqk', query_part, key_part) / math.sqrt(head_size)
    penalty = jnp.where(alive_keys > 0, jnp.float32(0.0), jnp.float32(MASKED))
    scores = scores + penalty[:, None, None, :]
    weights = jax.nn.softmax(scores, axis=-1).astype(jnp.bfloat16)
    mixture = jnp.einsum('whqk,wkhd->wqhd', weights.astype(jnp.float32), value_part)
    return mixture.astype(jnp.bfloat16).reshape(length, feat_width)

def reference(atom_single, positions, noise_index, token_counts, token_single, pair_repr, w_pos, atom_wq, atom_wk, atom_wv, atom_wo, w_pool, trans_w1, trans_w2, w_bias, token_wq, token_wk, token_wv, token_wo, w_back):
    highest = lax.Precision.HIGHEST
    run_count = NTOK // TOK_DEV
    counts = token_counts.reshape(run_count, TOK_DEV)
    token_ends = jnp.cumsum(counts, axis=1)
    slot_ids = jnp.arange(ATOM_DEV, dtype=jnp.int32)
    owner_token = lax.optimization_barrier(jnp.sum((slot_ids[None, :, None] >= token_ends[:, None, :]).astype(jnp.int32), axis=2))
    alive_slot = slot_ids[None, :] < token_ends[:, -1:]
    onehot = (owner_token[:, :, None] == jnp.arange(TOK_DEV, dtype=jnp.int32)[None, None, :]).astype(jnp.float32)
    noise_gain = noise_scale(noise_index)
    lifted = lax.dot_general(positions * noise_gain, w_pos, (((0,), (0,)), ((), ())), precision=highest)
    initial = atom_single.astype(jnp.float32) + lifted
    normed = normalize(initial).astype(jnp.bfloat16)
    queries = jnp.dot(normed, atom_wq, preferred_element_type=jnp.float32).astype(jnp.bfloat16)
    keyvals = jnp.dot(normed, jnp.concatenate([atom_wk, atom_wv], axis=1), preferred_element_type=jnp.float32).astype(jnp.bfloat16)
    margin = (WIN_K - WIN_Q) // 2
    padded_kv = jnp.pad(keyvals, ((margin, margin), (0, 0)))
    padded_live = jnp.pad(alive_slot.reshape(-1).astype(jnp.bfloat16), (margin, margin))
    mixture = window_attention(queries, padded_kv, padded_live, H_A)
    atom_state = initial + jnp.dot(mixture, atom_wo, preferred_element_type=jnp.float32)
    features = jax.nn.relu(jnp.dot(atom_state.astype(jnp.bfloat16), w_pool, preferred_element_type=jnp.float32))
    token_sums = jnp.einsum('bat,bac->btc', onehot, features.reshape(run_count, ATOM_DEV, C_S), precision=highest)
    pooled = token_sums.reshape(NTOK, C_S) / token_counts.astype(jnp.float32)[:, None]
    token_in = token_single.astype(jnp.float32) + pooled
    rows_per = math.gcd(NTOK, 16)

    def process(pair_rows):
        return pair_block(pair_rows, trans_w1, trans_w2, w_bias)
    pair_out, pair_bias = lax.map(process, pair_repr.reshape(NTOK // rows_per, rows_per, NTOK, C_Z))
    pair_out = pair_out.reshape(NTOK, NTOK, C_Z)
    pair_bias = pair_bias.transpose(1, 0, 2, 3).reshape(H_T, NTOK, NTOK)
    token_normed = normalize(token_in).astype(jnp.bfloat16)
    head_size = C_S // H_T
    token_queries = jnp.dot(token_normed, token_wq, preferred_element_type=jnp.float32).astype(jnp.bfloat16)
    token_kv = jnp.dot(token_normed, jnp.concatenate([token_wk, token_wv], axis=1), preferred_element_type=jnp.float32).astype(jnp.bfloat16)
    query_part = token_queries.reshape(NTOK, H_T, head_size).astype(jnp.float32)
    key_part = token_kv[:, :C_S].reshape(NTOK, H_T, head_size).astype(jnp.float32)
    value_part = token_kv[:, C_S:].reshape(NTOK, H_T, head_size).astype(jnp.float32)
    scores = jnp.einsum('ihd,jhd->hij', query_part, key_part) / math.sqrt(head_size)
    scores = scores + pair_bias.astype(jnp.float32)
    weights = jax.nn.softmax(scores, axis=-1).astype(jnp.bfloat16)
    token_mix = jnp.einsum('hij,jhd->ihd', weights.astype(jnp.float32), value_part).astype(jnp.bfloat16).reshape(NTOK, C_S)
    token_new = token_in + jnp.dot(token_mix, token_wo, preferred_element_type=jnp.float32)
    returned = jnp.dot(token_new.astype(jnp.bfloat16), w_back, preferred_element_type=jnp.float32)
    spread = jnp.einsum('bat,btc->bac', onehot, returned.reshape(run_count, TOK_DEV, C_A), precision=highest)
    atom_out = jnp.where(alive_slot.reshape(-1)[:, None], atom_state + spread.reshape(NATOM, C_A), jnp.float32(0.0))
    return (atom_out.astype(jnp.bfloat16), pair_out)
```

```python
import math

import jax
import jax.numpy as jnp
from jax import lax
from jax.experimental import pallas as pl
from jax.experimental.pallas import tpu as pltpu
from jax.sharding import PartitionSpec as P

H_A = 4
H_T = 16
WIN_Q = 32
WIN_K = 128
MARGIN = (WIN_K - WIN_Q) // 2
STEPS = 200
EPS = 1e-05
SIGMA_DATA = 16.0
SIGMA_MAX = 160.0
SIGMA_MIN = 0.0004
RHO = 7
MASKED = -1000000000.0

NY = 4
NZ = 8
NK = 2
NC = 4

ATOMS = 512
TOKS = 32
C_A = 128
C_S = 768
GROUP = 4
HEAD = 48
GW = GROUP * HEAD
ROWS = 8
COLS = 512

F32 = jnp.float32
BF = jnp.bfloat16
VMEM = pltpu.CompilerParams(vmem_limit_bytes=56 * 2**20)


def dot(a, b):
    return jnp.dot(a, b, preferred_element_type=F32)


def dot_nt(a, b):
    return lax.dot_general(a, b, (((1,), (1,)), ((), ())), preferred_element_type=F32)


def iota(shape, dim):
    return lax.broadcasted_iota(jnp.int32, shape, dim)


def hi_lo(v):
    hi = v.astype(BF)
    return hi, (v - hi.astype(F32)).astype(BF)


def three(v):
    hi = v.astype(BF)
    rest = v - hi.astype(F32)
    mid = rest.astype(BF)
    return hi, mid, (rest - mid.astype(F32)).astype(BF)


def normalize(values):
    average = jnp.mean(values, axis=-1, keepdims=True)
    centred = values - average
    variance = jnp.mean(centred * centred, axis=-1, keepdims=True)
    return centred * lax.rsqrt(variance + EPS)


def call(kernel, outs, *args, name, flops=0, smem=()):
    vm = pl.BlockSpec(memory_space=pltpu.VMEM)
    sm = pl.BlockSpec(memory_space=pltpu.SMEM)
    return pl.pallas_call(
        kernel,
        in_specs=[sm if i in smem else vm for i in range(len(args))],
        out_specs=[vm] * len(outs),
        out_shape=[jax.ShapeDtypeStruct(s, d) for s, d in outs],
        compiler_params=VMEM,
        cost_estimate=pl.CostEstimate(flops=flops, bytes_accessed=2**20, transcendentals=0),
        name=name,
    )(*args)


def atom_in_kernel(noise_ref, pos_ref, wpos_ref, single_ref, counts_ref, initial_ref, normed_ref, first_ref, last_ref):
    level = jnp.full((1, C_A), noise_ref[0], jnp.int32).astype(F32)
    upper = SIGMA_MAX ** (1.0 / RHO)
    lower = SIGMA_MIN ** (1.0 / RHO)
    root = upper + level / (STEPS - 1) * (lower - upper)
    square = root * root
    sigma = square * square * square * root
    gain = 1.0 / jnp.sqrt(sigma * sigma + SIGMA_DATA * SIGMA_DATA)
    lifted = lax.dot_general(
        pos_ref[...], wpos_ref[...] * gain, (((0,), (0,)), ((), ())),
        precision=lax.Precision.HIGHEST, preferred_element_type=F32,
    )
    initial = single_ref[...].astype(F32) + lifted
    initial_ref[...] = initial
    normed = normalize(initial).astype(BF)
    normed_ref[...] = normed
    total = jnp.sum(counts_ref[...], axis=1, keepdims=True)
    slots = iota((ATOMS, C_A), 0)
    live = jnp.where(slots < total, 1.0, 0.0).astype(BF)
    both = jnp.concatenate([normed, live], axis=1)
    first_ref[...] = both[:MARGIN]
    last_ref[...] = both[ATOMS - MARGIN :]


def spans(counts_ref):
    row = counts_ref[...].astype(F32)
    grid = jnp.broadcast_to(row, (TOKS, TOKS))
    r, c = iota((TOKS, TOKS), 0), iota((TOKS, TOKS), 1)
    count_col = jnp.sum(jnp.where(r == c, grid, 0.0), axis=1, keepdims=True)
    end_col = jnp.sum(jnp.where(c <= r, grid, 0.0), axis=1, keepdims=True)
    end_row = jnp.sum(jnp.where(r <= c, jnp.broadcast_to(count_col, (TOKS, TOKS)), 0.0), axis=0, keepdims=True)
    return row, count_col, end_row, end_col


def atom_mid_kernel(
    normed_ref, initial_ref, before_ref, after_ref, counts_ref,
    wq_ref, wk_ref, wv_ref, wo_ref, pool_ref, single_ref, twq_ref, twk_ref,
    state_ref, token_in_ref, token_normed_ref, t_ref,
):
    before = before_ref[...]
    after = after_ref[...]
    normed = normed_ref[...]
    _, count_col, _, end_col = spans(counts_ref)
    slots = iota((TOKS, ATOMS), 1).astype(F32)
    onehot = jnp.where((slots < end_col) & (slots >= end_col - count_col), 1.0, 0.0).astype(BF)
    total = jnp.sum(counts_ref[...], axis=1, keepdims=True)
    own_live = jnp.where(iota((ATOMS, C_A), 0) < total, 1.0, 0.0).astype(BF)
    wide = jnp.concatenate([before[:, :C_A], normed, after[:, :C_A]], axis=0)
    live = jnp.concatenate([before[:, C_A:], own_live, after[:, C_A:]], axis=0)
    queries = dot(normed, wq_ref[...]).astype(BF)
    keys = dot(wide, wk_ref[...]).astype(BF)
    values = dot(wide, wv_ref[...]).astype(BF)
    lane_head = iota((H_A * WIN_Q, C_A), 1) // (C_A // H_A)
    row_head = iota((H_A * WIN_Q, C_A), 0) // WIN_Q
    mine = lane_head == row_head
    eye = jnp.where(iota((WIN_K, WIN_K), 0) == iota((WIN_K, WIN_K), 1), 1.0, 0.0).astype(BF)
    scale = 1.0 / math.sqrt(C_A // H_A)
    mixes = []
    for w in range(ATOMS // WIN_Q):
        q = queries[w * WIN_Q : (w + 1) * WIN_Q]
        q4 = jnp.where(mine, jnp.concatenate([q] * H_A, axis=0).astype(F32), 0.0).astype(BF)
        lo = w * WIN_Q
        k = keys[lo : lo + WIN_K]
        v = values[lo : lo + WIN_K]
        alive = dot_nt(jnp.ones((8, C_A), BF), jnp.where(iota((WIN_K, C_A), 1) == 0, live[lo : lo + WIN_K].astype(F32), 0.0).astype(BF))
        scores = dot_nt(q4, k) * scale + jnp.where(alive[:1] > 0.5, 0.0, MASKED)
        top = jnp.max(scores, axis=1, keepdims=True)
        p = jnp.exp(scores - top)
        weight = (p / jnp.sum(p, axis=1, keepdims=True)).astype(BF)
        o = jnp.where(mine, dot(weight, v), 0.0)
        mixes.append(o[:32] + o[32:64] + o[64:96] + o[96:])
    mix = jnp.concatenate(mixes, axis=0).astype(BF)
    state = initial_ref[...] + dot(mix, wo_ref[...])
    state_ref[...] = state
    features = jnp.maximum(dot(state.astype(BF), pool_ref[...]), 0.0)
    f_hi, f_lo = hi_lo(features)
    sums = dot(onehot, f_hi) + dot(onehot, f_lo)
    token_in = single_ref[...].astype(F32) + sums / count_col
    token_in_ref[...] = token_in
    token_normed = normalize(token_in).astype(BF)
    token_normed_ref[...] = token_normed
    tq = dot(token_normed, twq_ref[...]).astype(BF).astype(F32)
    lanes = iota((ROWS, GW), 1) // HEAD
    pieces = [
        jnp.where(lanes == h, tq[ib * ROWS : (ib + 1) * ROWS], 0.0)
        for ib in range(TOKS // ROWS)
        for h in range(GROUP)
    ]
    spread = jnp.concatenate(pieces, axis=0).astype(BF)
    t_ref[...] = (dot_nt(spread, twk_ref[...]) * (1.0 / math.sqrt(HEAD))).astype(BF)


def pair_kernel(x_ref, w1_ref, w2_ref, wb_ref, *refs, fresh):
    if not fresh:
        refs = refs[2:]
    out_ref, bias_ref, cen_s, avg_s, w1_s, w2_s, wb_s, vb_s = refs
    pairs = ROWS // 2

    @pl.when(pl.program_id(0) == 0)
    def _():
        r, c = iota((256, 256), 0), iota((256, 256), 1)
        same = (r // 128) == (c // 128)
        avg_s[...] = jnp.where(same, 1.0 / 128, 0.0).astype(BF)
        cen_s[...] = (jnp.where(r == c, 1.0, 0.0) - jnp.where(same, 1.0 / 128, 0.0)).astype(BF)
        w1_s[:, :256] = w1_ref[:, :256] * jnp.asarray(0.5, BF)
        w1_s[:, 256:] = w1_ref[:, 256:]
        w2 = w2_ref[...]
        w2_s[:, :128] = w2
        wide = w2.astype(F32)
        w2_s[:, 128:] = (wide - jnp.mean(wide, axis=1, keepdims=True)).astype(BF)
        head, lane = iota((H_T, 128), 0), iota((H_T, 128), 1)
        spot = iota((128, 128), 1)
        for p in range(pairs):
            for k in range(2):
                g = k * pairs + p
                place = jnp.where(lane == head * ROWS + g, 1.0, 0.0).astype(BF)
                wb_s[p, 128 * k : 128 * k + 128, :] = dot(wb_ref[...], place).astype(BF)
                vb_s[p, 128 * k : 128 * k + 128, :] = jnp.where(spot % ROWS == g, 1.0 / 128, 0.0).astype(BF)

    m = pairs * COLS
    xs = [x_ref[:pairs].reshape(m, 128), x_ref[pairs:].reshape(m, 128)]
    c = dot(jnp.concatenate(xs, axis=1), cen_s[...])
    v = dot((c * c).astype(BF), avg_s[...])
    n = (c * lax.rsqrt(v + EPS)).astype(BF)
    kept, squares = [], []
    for k in range(2):
        g = dot(n[:, 128 * k : 128 * k + 128], w1_s[...])
        gate, up = g[:, :256], g[:, 256:]
        h = ((gate + gate * jnp.tanh(gate)) * up).astype(BF)
        u = dot(h, w2_s[...])
        out_ref[k * pairs : (k + 1) * pairs] = (
            (xs[k].astype(F32) + u[:, :128]).astype(BF).reshape(pairs, COLS, 128)
        )
        c2 = c[:, 128 * k : 128 * k + 128] + u[:, 128:]
        kept.append(c2.astype(BF))
        squares.append((c2 * c2).astype(BF))
    cc = jnp.concatenate(kept, axis=1)
    ss = jnp.concatenate(squares, axis=1)
    acc = jnp.zeros((COLS, 128), F32)
    var = jnp.zeros((COLS, 128), F32)
    for p in range(pairs):
        acc = acc + dot(cc[p * COLS : (p + 1) * COLS], wb_s[p])
        var = var + dot(ss[p * COLS : (p + 1) * COLS], vb_s[p])
    b = acc * lax.rsqrt(var + EPS)
    bias_ref[...] = b.T.astype(BF).reshape(NC, 1, GROUP * ROWS, COLS)


def pair_call(x, w1, w2, wb, prior, start, count):
    fresh = prior is None
    whole = lambda a: pl.BlockSpec(a.shape, lambda i: (0,) * a.ndim)
    anywhere = pl.BlockSpec(memory_space=pl.ANY)
    n = TOKS // ROWS
    return pl.pallas_call(
        lambda *refs: pair_kernel(*refs, fresh=fresh),
        grid=(count,),
        in_specs=[pl.BlockSpec((ROWS, COLS, 128), lambda i: (i + start, 0, 0)), whole(w1), whole(w2), whole(wb)]
        + ([] if fresh else [anywhere] * 2),
        out_specs=[
            pl.BlockSpec((ROWS, COLS, 128), lambda i: (i + start, 0, 0)),
            pl.BlockSpec((NC, 1, GROUP * ROWS, COLS), lambda i: (0, i + start, 0, 0)),
        ],
        out_shape=[
            jax.ShapeDtypeStruct(x.shape, BF),
            jax.ShapeDtypeStruct((NC, n, GROUP * ROWS, COLS), BF),
        ],
        scratch_shapes=[
            pltpu.VMEM((256, 256), BF),
            pltpu.VMEM((256, 256), BF),
            pltpu.VMEM((128, 512), BF),
            pltpu.VMEM((256, 256), BF),
            pltpu.VMEM((ROWS // 2, 256, 128), BF),
            pltpu.VMEM((ROWS // 2, 256, 128), BF),
        ],
        input_output_aliases={} if fresh else {4: 0, 5: 1},
        compiler_params=VMEM,
        cost_estimate=pl.CostEstimate(flops=count * 3 * 10**9, bytes_accessed=count * 2**21, transcendentals=0),
        name="pair",
    )(x, w1, w2, wb, *(() if fresh else prior))


def weights_kernel(wv_ref, wo_ref, back_ref, out_ref):
    out_ref[:C_S, :GW] = wv_ref[...]
    out_ref[:C_S, GW:] = jnp.zeros((C_S, 256 - GW), BF)
    hi, lo = hi_lo(dot(wo_ref[...], back_ref[...]))
    out_ref[C_S:, :C_A] = hi
    out_ref[C_S:, C_A:] = lo


def attention_kernel(
    place_ref, t0, t1, t2, t3, own_ref, other_ref, bias_ref, w0, w1, w2, w3, msg_ref, back_ref, xk_s, o_s
):
    col, core = place_ref[0], place_ref[1]
    xk_s[:, pl.ds(core, 1)] = own_ref[...].reshape(NZ, 1, TOKS, C_S)
    xk_s[:, pl.ds(1 - core, 1)] = other_ref[...].reshape(NZ, 1, TOKS, C_S)
    xk = xk_s[...].reshape(COLS, C_S)
    wide = GROUP * TOKS
    t = jnp.concatenate([t0[...], t1[...], t2[...], t3[...]], axis=0)
    scores = dot_nt(t, xk)
    groups = [(col + NC - s) % NC for s in range(NC)]
    scores = jnp.concatenate(
        [
            scores[s * wide : (s + 1) * wide] + bias_ref[pl.ds(groups[s], 1)].reshape(wide, COLS).astype(F32)
            for s in range(NC)
        ],
        axis=0,
    )
    top = jnp.max(scores, axis=1, keepdims=True)
    p = jnp.exp(scores - top)
    total = jnp.sum(p, axis=1, keepdims=True)
    mixed = (dot(p.astype(BF), xk) / total).astype(BF)
    blocks = TOKS // ROWS
    lane_head = iota((1, GROUP, 1, 256), 3) // HEAD
    row_head = iota((1, GROUP, 1, 256), 1)
    lane16 = iota((1, GROUP, 1, 128), 3) % H_T
    row16 = iota((1, GROUP, 1, 128), 1)
    tops = jnp.zeros((TOKS, 128), F32)
    totals = jnp.zeros((TOKS, 128), F32)
    for s, w in enumerate((w0, w1, w2, w3)):
        lo = s * wide
        o = dot(mixed[lo : lo + wide], w[:C_S, :]).reshape(blocks, GROUP, ROWS, 256)
        o = jnp.sum(jnp.where(lane_head == row_head, o, 0.0), axis=1).reshape(TOKS, 256)
        o_s[pl.ds(groups[s], 1)] = o.reshape(1, TOKS, 256)
        back_ref[pl.ds(groups[s], 1)] = w[C_S:, :].reshape(1, GW, 256)
        here = lane16 == row16 + groups[s] * GROUP
        for value, which in ((top, 0), (total, 1)):
            part = jnp.broadcast_to(value[lo : lo + wide], (wide, 128)).reshape(blocks, GROUP, ROWS, 128)
            part = jnp.sum(jnp.where(here, part, 0.0), axis=1).reshape(TOKS, 128)
            if which == 0:
                tops = tops + part
            else:
                totals = totals + part
    part_of = iota((TOKS, 128), 1) // H_T
    stats = jnp.zeros((TOKS, 128), F32)
    for i, piece in enumerate((*three(tops), *three(totals))):
        stats = jnp.where(part_of == i, piece.astype(F32), stats)
    msg_ref[...] = jnp.concatenate([o_s[g][:, :GW] for g in range(NC)] + [stats], axis=1).astype(BF)


def final_kernel(m0, m1, m2, m3, token_in_ref, state_ref, counts_ref, wback_ref, back_ref, out_ref):
    msgs = [m0[...], m1[...], m2[...], m3[...]]
    r, c = iota((128, 256), 0), iota((128, 256), 1)
    pick = ((r // H_T) // 3 == c // 128) & (r % H_T == c % H_T) & (r < 6 * H_T)
    stats = dot(jnp.concatenate([m[:, C_S:] for m in msgs], axis=0), jnp.where(pick, 1.0, 0.0).astype(BF))
    tops = [stats[i * TOKS : (i + 1) * TOKS, :128] for i in range(NC)]
    totals = [stats[i * TOKS : (i + 1) * TOKS, 128:] for i in range(NC)]
    top = jnp.maximum(jnp.maximum(tops[0], tops[1]), jnp.maximum(tops[2], tops[3]))
    shares = [l * jnp.exp(t - top) for l, t in zip(totals, tops)]
    whole = shares[0] + shares[1] + shares[2] + shares[3]
    r, c = iota((128, C_S), 0), iota((128, C_S), 1)
    expand = jnp.where((r % H_T == c // HEAD) & (r < 2 * H_T), 1.0, 0.0).astype(BF)
    part_of = iota((TOKS, 128), 1) // H_T
    coefs = []
    for share in shares:
        hi, lo = hi_lo(share / whole)
        coefs.append(jnp.where(part_of == 0, hi.astype(F32), lo.astype(F32)).astype(BF))
    scale = dot(jnp.concatenate(coefs, axis=0), expand)
    mix = jnp.zeros((TOKS, C_S), F32)
    for i, m in enumerate(msgs):
        mix = mix + scale[i * TOKS : (i + 1) * TOKS] * m[:, :C_S].astype(F32)
    folded = dot(mix.astype(BF), back_ref[...].reshape(C_S, 256))
    returned = dot(token_in_ref[...].astype(BF), wback_ref[...]) + folded[:, :C_A] + folded[:, C_A:]
    row, _, end_row, _ = spans(counts_ref)
    slots = iota((ATOMS, TOKS), 0).astype(F32)
    onehot = jnp.where((slots < end_row) & (slots >= end_row - row), 1.0, 0.0).astype(BF)
    r_hi, r_lo = hi_lo(returned)
    spread = dot(onehot, r_hi) + dot(onehot, r_lo)
    alive = iota((ATOMS, C_A), 0) < jnp.sum(counts_ref[...], axis=1, keepdims=True)
    out_ref[...] = jnp.where(alive, state_ref[...] + spread, 0.0).astype(BF)


def around(array, axis, size):
    return [lax.ppermute(array, axis, [(i, (i + s) % size) for i in range(size)]) for s in range(1, size)]


def local(
    atom_single, positions, noise_index, token_counts, token_single, pair_repr, w_pos, atom_wq, atom_wk, atom_wv,
    atom_wo, w_pool, trans_w1, trans_w2, w_bias, token_wq, token_wk, token_wv, token_wo, w_back,
):
    atoms = NY * NZ * NK
    counts = token_counts.reshape(1, TOKS)
    col = lax.axis_index("col")
    place = jnp.stack([col, lax.axis_index("atom") % NK]).astype(jnp.int32)

    initial, normed, first, last = call(
        atom_in_kernel,
        [((ATOMS, C_A), F32), ((ATOMS, C_A), BF), ((MARGIN, 2 * C_A), BF), ((MARGIN, 2 * C_A), BF)],
        noise_index, positions, w_pos, atom_single, counts, name="atom_in", smem=(0,), flops=10**8,
    )
    before = lax.ppermute(last, "atom", [(i, i + 1) for i in range(atoms - 1)])
    after = lax.ppermute(first, "atom", [(i + 1, i) for i in range(atoms - 1)])
    (packed,) = call(
        weights_kernel, [((C_S + GW, 256), BF)], token_wv, token_wo, w_back, name="weights", flops=10**8
    )
    weights = [packed] + around(packed, "col", NC)
    state, token_in, token_normed, t_own = call(
        atom_mid_kernel,
        [((ATOMS, C_A), F32), ((TOKS, C_S), F32), ((TOKS, C_S), BF), ((GROUP * TOKS, C_S), BF)],
        normed, initial, before, after, counts, atom_wq, atom_wk, atom_wv, atom_wo, w_pool, token_single,
        token_wq, token_wk, name="atom_mid", flops=10**9,
    )
    flip = [
        ((y * NZ * NK + i) * NC + x, (x * NZ * NK + i) * NC + y)
        for y in range(NY) for i in range(NZ * NK) for x in range(NC)
    ]
    turned = lax.ppermute(token_normed, ("atom", "col"), flip)
    lines = [[(y * NZ + z) * NK + k for z in range(NZ)] for y in range(NY) for k in range(NK)]
    own = lax.all_to_all(
        jnp.broadcast_to(turned[None], (NZ, TOKS, C_S)), "atom", 0, 0, axis_index_groups=lines, tiled=True
    )
    other = lax.ppermute(own, "atom", [(i, i ^ 1) for i in range(atoms)])
    queries = [t_own] + around(t_own, "col", NC)

    prior = None
    for start in range(TOKS // ROWS):
        prior = pair_call(pair_repr, trans_w1, trans_w2, w_bias, prior, start, 1)
    pair_out, bias = prior

    msg, back = pl.pallas_call(
        attention_kernel,
        in_specs=[pl.BlockSpec(memory_space=pltpu.SMEM)] + [pl.BlockSpec(memory_space=pltpu.VMEM)] * 11,
        out_specs=[pl.BlockSpec(memory_space=pltpu.VMEM)] * 2,
        out_shape=[
            jax.ShapeDtypeStruct((TOKS, C_S + 128), BF),
            jax.ShapeDtypeStruct((NC, GW, 256), BF),
        ],
        scratch_shapes=[pltpu.VMEM((NZ, NK, TOKS, C_S), BF), pltpu.VMEM((NC, TOKS, 256), F32)],
        compiler_params=VMEM,
        cost_estimate=pl.CostEstimate(flops=3 * 10**9, bytes_accessed=2**20, transcendentals=0),
        name="attention",
    )(place, *queries, own, other, bias.reshape(NC, GROUP * TOKS, COLS), *weights)
    msgs = [msg] + around(msg, "col", NC)
    (atom_out,) = call(
        final_kernel, [((ATOMS, C_A), BF)], *msgs, token_in, state, counts, w_back, back, name="final", flops=10**8
    )
    return (atom_out, pair_out)


def solution(mesh):
    placed = (
        P("atom", None), P(None, "atom"), P(), P("atom"), P("atom", None), P("atom", "col", None),
        P(), P(), P(), P(), P(), P(), P(), P(), P(),
        P(None, "col"), P(None, "col"), P(None, "col"), P("col", None), P(),
    )
    return jax.shard_map(
        local,
        mesh=mesh,
        in_specs=placed,
        out_specs=(P("atom", None), P("atom", "col", None)),
        check_vma=False,
    )
```

```python
import math

import jax
import jax.numpy as jnp
from jax import lax
from jax.experimental import pallas as pl
from jax.experimental.pallas import tpu as pltpu
from jax.sharding import PartitionSpec as P

H_A = 4
H_T = 16
WIN_Q = 32
WIN_K = 128
MARGIN = (WIN_K - WIN_Q) // 2
STEPS = 200
EPS = 1e-05
SIGMA_DATA = 16.0
SIGMA_MAX = 160.0
SIGMA_MIN = 0.0004
RHO = 7
MASKED = -1000000000.0

NY = 4
NZ = 8
NK = 2
NC = 4

ATOMS = 512
TOKS = 32
C_A = 128
C_S = 768
GROUP = 4
HEAD = 48
GW = GROUP * HEAD
FOLD = GW * C_A // C_S
ROWS = 8
COLS = 512
CHUNKS = ((0, 1), (1, 2), (3, 1))

F32 = jnp.float32
BF = jnp.bfloat16


def dot(a, b):
    return jnp.dot(a, b, preferred_element_type=F32)


def dot_nt(a, b):
    return lax.dot_general(a, b, (((1,), (1,)), ((), ())), preferred_element_type=F32)


def iota(shape, dim):
    return lax.broadcasted_iota(jnp.int32, shape, dim)


def hi_lo(v):
    hi = v.astype(BF)
    return hi, (v - hi.astype(F32)).astype(BF)


def three(v):
    hi = v.astype(BF)
    rest = v - hi.astype(F32)
    mid = rest.astype(BF)
    return hi, mid, (rest - mid.astype(F32)).astype(BF)


def normalize(values):
    average = jnp.mean(values, axis=-1, keepdims=True)
    centred = values - average
    variance = jnp.mean(centred * centred, axis=-1, keepdims=True)
    return centred * lax.rsqrt(variance + EPS)


class Fetched:
    def __init__(self, copy, buffer):
        self.copy, self.buffer, self.here, self.shape = copy, buffer, False, buffer.shape

    def arrive(self):
        if not self.here:
            self.copy.wait()
            self.here = True

    def __getitem__(self, index):
        self.arrive()
        return self.buffer[index]


class Sent:
    def __init__(self, copy, buffer):
        self.copy, self.buffer, self.gone = copy, buffer, False

    def __setitem__(self, index, value):
        self.buffer[index] = value

    def send(self):
        if not self.gone:
            self.copy.start()
            self.gone = True


def call(kernel, outs, args, *, name, smem=(), scratch=(), far=(), aliases=None, flops=0):
    n, m, k = len(args), len(outs), len(scratch)
    fetch = [i for i in range(n) if i not in smem and i not in far]
    send = [i for i in range(m) if n + i not in far]

    def body(*refs):
        ins, given, rest = list(refs[:n]), list(refs[n : n + m]), refs[n + m : n + m + k]
        buffers, sems = refs[n + m + k : -1], refs[-1]
        for slot, i in enumerate(fetch):
            copy = pltpu.make_async_copy(ins[i], buffers[slot], sems.at[slot])
            copy.start()
            ins[i] = Fetched(copy, buffers[slot])
        for slot, i in enumerate(send, len(fetch)):
            given[i] = Sent(pltpu.make_async_copy(buffers[slot], given[i], sems.at[slot]), buffers[slot])
        kernel(*ins, *given, *rest)
        for i in fetch:
            ins[i].arrive()
        for i in send:
            given[i].send()
        for i in send:
            given[i].copy.wait()

    return pl.pallas_call(
        body,
        in_specs=[pl.BlockSpec(memory_space=pltpu.SMEM if i in smem else pltpu.HBM) for i in range(n)],
        out_specs=[pl.BlockSpec(memory_space=pltpu.HBM)] * m,
        out_shape=[jax.ShapeDtypeStruct(s, d) for s, d in outs],
        scratch_shapes=[
            *scratch,
            *(pltpu.VMEM(args[i].shape, args[i].dtype) for i in fetch),
            *(pltpu.VMEM(*outs[i]) for i in send),
            pltpu.SemaphoreType.DMA((max(len(fetch) + len(send), 1),)),
        ],
        input_output_aliases=aliases or {},
        compiler_params=pltpu.CompilerParams(vmem_limit_bytes=56 * 2**20),
        cost_estimate=pl.CostEstimate(flops=flops, bytes_accessed=1024, transcendentals=0),
        name=name,
    )(*args)


def atom_in_kernel(
    noise_ref, pos_ref, wpos_ref, single_ref, counts_ref, initial_ref, normed_ref, inner_ref, outer_ref
):
    level = jnp.full((1, C_A), noise_ref[0], jnp.int32).astype(F32)
    upper = SIGMA_MAX ** (1.0 / RHO)
    lower = SIGMA_MIN ** (1.0 / RHO)
    root = upper + level / (STEPS - 1) * (lower - upper)
    square = root * root
    sigma = square * square * square * root
    gain = 1.0 / jnp.sqrt(sigma * sigma + SIGMA_DATA * SIGMA_DATA)
    lifted = lax.dot_general(
        pos_ref[...], wpos_ref[...] * gain, (((0,), (0,)), ((), ())),
        precision=lax.Precision.HIGHEST, preferred_element_type=F32,
    )
    initial = single_ref[...].astype(F32) + lifted
    normed = normalize(initial).astype(BF)
    total = jnp.sum(counts_ref[...], axis=1, keepdims=True)
    slots = iota((ATOMS, C_A), 0)
    live = jnp.where(slots < total, 1.0, 0.0).astype(BF)
    both = jnp.concatenate([normed, live], axis=1)
    first, last = both[:MARGIN].astype(F32), both[ATOMS - MARGIN :].astype(F32)
    lower = lax.axis_index("atom") % NK == 0
    inner_ref[...] = jnp.where(lower, last, first).astype(BF)
    inner_ref.send()
    outer_ref[...] = jnp.where(lower, first, last).astype(BF)
    outer_ref.send()
    normed_ref[...] = normed
    normed_ref.send()
    initial_ref[...] = initial
    initial_ref.send()


def pack_kernel(twv_ref, two_ref, back_ref, _, packed_ref):
    folded = dot(two_ref[...], back_ref[...]).astype(BF)
    packed_ref[GW:, :] = jnp.concatenate(
        [folded[i * FOLD : (i + 1) * FOLD] for i in range(GW // FOLD)], axis=1
    )
    packed_ref[:GW, :] = twv_ref[...]


def spans(counts_ref):
    row = counts_ref[...].astype(F32)
    grid = jnp.broadcast_to(row, (TOKS, TOKS))
    r, c = iota((TOKS, TOKS), 0), iota((TOKS, TOKS), 1)
    count_col = jnp.sum(jnp.where(r == c, grid, 0.0), axis=1, keepdims=True)
    end_col = jnp.sum(jnp.where(c <= r, grid, 0.0), axis=1, keepdims=True)
    end_row = jnp.sum(jnp.where(r <= c, jnp.broadcast_to(count_col, (TOKS, TOKS)), 0.0), axis=0, keepdims=True)
    return row, count_col, end_row, end_col


def atom_mid_kernel(
    normed_ref, inner_ref, outer_ref, counts_ref, wq_ref, wk_ref, wv_ref, initial_ref, wo_ref, pool_ref,
    single_ref, twq_ref, twk_ref, state_ref, token_in_ref, token_normed_ref, t_ref,
):
    lower = lax.axis_index("atom") % NK == 0
    inner, outer = inner_ref[...].astype(F32), outer_ref[...].astype(F32)
    before = jnp.where(lower, outer, inner).astype(BF)
    after = jnp.where(lower, inner, outer).astype(BF)
    normed = normed_ref[...]
    _, count_col, _, end_col = spans(counts_ref)
    slots = iota((TOKS, ATOMS), 1).astype(F32)
    onehot = jnp.where((slots < end_col) & (slots >= end_col - count_col), 1.0, 0.0).astype(BF)
    wide = jnp.concatenate([before[:, :C_A], normed, after[:, :C_A]], axis=0)
    n_before = jnp.sum(before[:, C_A:].astype(F32), axis=0, keepdims=True)
    n_after = jnp.sum(after[:, C_A:].astype(F32), axis=0, keepdims=True)
    n_own = jnp.sum(counts_ref[...].astype(F32), axis=1, keepdims=True)
    queries = dot(normed, wq_ref[...]).astype(BF)
    keys = dot(wide, wk_ref[...]).astype(BF)
    values = dot(wide, wv_ref[...]).astype(BF)
    stacked = H_A * WIN_Q
    mine = iota((stacked, C_A), 1) // (C_A // H_A) == iota((stacked, C_A), 0) // WIN_Q
    pick = jnp.where(mine, 1.0, 0.0).astype(BF)
    scale = 1.0 / math.sqrt(C_A // H_A)
    windows = ATOMS // WIN_Q
    scores = []
    for w in range(windows):
        q = queries[w * WIN_Q : (w + 1) * WIN_Q]
        q4 = jnp.concatenate([q] * H_A, axis=0) * pick
        slot = (iota((1, WIN_K), 1) + (w * WIN_Q - MARGIN)).astype(F32)
        bound = jnp.broadcast_to(n_own, (1, WIN_K))
        if w * WIN_Q < MARGIN:
            bound = jnp.where(slot < 0, n_before - MARGIN, bound)
        if w * WIN_Q - MARGIN + WIN_K > ATOMS:
            bound = jnp.where(slot >= ATOMS, n_after + ATOMS, bound)
        penalty = jnp.where(slot < bound, 0.0, MASKED)
        scores.append(dot_nt(q4, keys[w * WIN_Q : w * WIN_Q + WIN_K]) * scale + penalty)
    scores = jnp.concatenate(scores, axis=0)
    p = jnp.exp(scores - jnp.max(scores, axis=1, keepdims=True))
    weight = (p / jnp.sum(p, axis=1, keepdims=True)).astype(BF)
    mixes = []
    for w in range(windows):
        o = dot(weight[w * stacked : (w + 1) * stacked], values[w * WIN_Q : w * WIN_Q + WIN_K])
        o = jnp.where(mine, o, 0.0)
        mixes.append(o[:32] + o[32:64] + o[64:96] + o[96:])
    mix = jnp.concatenate(mixes, axis=0).astype(BF)
    state = initial_ref[...] + dot(mix, wo_ref[...])
    state_ref[...] = state
    state_ref.send()
    features = jnp.maximum(dot(state.astype(BF), pool_ref[...]), 0.0)
    f_hi, f_lo = hi_lo(features)
    sums = dot(onehot, f_hi) + dot(onehot, f_lo)
    token_in = single_ref[...].astype(F32) + sums / count_col
    token_normed = normalize(token_in).astype(BF)
    token_normed_ref[...] = token_normed
    token_normed_ref.send()
    token_in_ref[...] = token_in
    token_in_ref.send()
    tq = dot_nt(token_normed, twq_ref[...]).astype(BF).astype(F32)
    lanes = iota((ROWS, GW), 1) // HEAD
    pieces = [
        jnp.where(lanes == h, tq[ib * ROWS : (ib + 1) * ROWS], 0.0)
        for ib in range(TOKS // ROWS)
        for h in range(GROUP)
    ]
    spread = jnp.concatenate(pieces, axis=0).astype(BF)
    t_ref[...] = (dot(spread, twk_ref[...]) * (1.0 / math.sqrt(HEAD))).astype(BF)


def pair_kernel(x_ref, w1_ref, w2_ref, wb_ref, *refs, start, count):
    out_ref, bias_ref, x_s, y_s, b_s, w1_s, w2_s, in_sem, out_sem, bias_sem = refs[-10:]
    pairs = ROWS // 2
    arrivals = [
        pltpu.make_async_copy(x_ref.at[pl.ds((start + i) * ROWS, ROWS)], x_s.at[i], in_sem.at[i])
        for i in range(count)
    ]
    leaving = [
        pltpu.make_async_copy(
            y_s.at[i, pl.ds(k * pairs, pairs)],
            out_ref.at[pl.ds((start + i) * ROWS + k * pairs, pairs)],
            out_sem.at[2 * i + k],
        )
        for i in range(count)
        for k in range(2)
    ]
    biases = [
        pltpu.make_async_copy(b_s.at[:, i], bias_ref.at[:, i], bias_sem.at[i]) for i in range(count)
    ]
    for copy in arrivals:
        copy.start()
    r, c = iota((256, 256), 0), iota((256, 256), 1)
    same = (r // 128) == (c // 128)
    centre = (jnp.where(r == c, 1.0, 0.0) - jnp.where(same, 1.0 / 128, 0.0)).astype(BF)
    w1_s[:, :256] = w1_ref[:, :256] * jnp.asarray(0.5, BF)
    w1_s[:, 256:] = w1_ref[:, 256:]
    w2 = w2_ref[...]
    w2_s[:, :128] = w2
    wide = w2.astype(F32)
    w2_s[:, 128:] = (wide - jnp.mean(wide, axis=1, keepdims=True)).astype(BF)
    head, lane = iota((H_T, 128), 0), iota((H_T, 128), 1)
    wb = wb_ref[...]
    heads = [
        lax.dot_general(
            wb, jnp.where(lane == head * ROWS + g, 1.0, 0.0).astype(BF), (((0,), (0,)), ((), ())),
            preferred_element_type=F32,
        ).astype(BF)
        for g in range(ROWS)
    ]
    heads = [jnp.concatenate([heads[p], heads[pairs + p]], axis=0) for p in range(pairs)]
    m = pairs * COLS
    for step in range(count):
        arrivals[step].wait()
        xs = [x_s[step, :pairs].reshape(m, 128), x_s[step, pairs:].reshape(m, 128)]
        c = dot(jnp.concatenate(xs, axis=1), centre)
        kept = []
        for k in range(2):
            ck = c[:, 128 * k : 128 * k + 128]
            n = (ck * lax.rsqrt(jnp.mean(ck * ck, axis=1, keepdims=True) + EPS)).astype(BF)
            g = dot(n, w1_s[...])
            gate, up = g[:, :256], g[:, 256:]
            h = ((gate + gate * jnp.tanh(gate)) * up).astype(BF)
            u = dot(h, w2_s[...])
            y_s[step, k * pairs : (k + 1) * pairs] = (
                (xs[k].astype(F32) + u[:, :128]).astype(BF).reshape(pairs, COLS, 128)
            )
            c2 = ck + u[:, 128:]
            kept.append((c2 * lax.rsqrt(jnp.mean(c2 * c2, axis=1, keepdims=True) + EPS)).astype(BF))
            leaving[2 * step + k].start()
        cc = jnp.concatenate(kept, axis=1)
        acc = jnp.zeros((COLS, 128), F32)
        for p in range(pairs):
            acc = acc + dot(cc[p * COLS : (p + 1) * COLS], heads[p])
        b_s[:, step] = acc.T.astype(BF).reshape(NC, GROUP * ROWS, COLS)
        biases[step].start()
    for copy in (*leaving, *biases):
        copy.wait()


def pair_call(x, w1, w2, wb, prior, after, start, count):
    block = (count, ROWS, COLS, 128)
    more = [a for a in (prior, after) if a is not None]
    n = 4 + len(more)
    return call(
        lambda *refs: pair_kernel(*refs, start=start, count=count),
        [(x.shape, BF), ((NC, count, GROUP * ROWS, COLS), BF)],
        (x, w1, w2, wb, *more),
        name="pair", far=(0, *range(4, n + 2)), aliases={} if prior is None else {4: 0},
        scratch=[
            pltpu.VMEM(block, BF), pltpu.VMEM(block, BF), pltpu.VMEM((NC, count, GROUP * ROWS, COLS), BF),
            pltpu.VMEM((128, 512), BF), pltpu.VMEM((256, 256), BF),
            *(pltpu.SemaphoreType.DMA((i * count,)) for i in (1, 2, 1)),
        ],
        flops=1000,
    )


def attention_kernel(
    t0, t1, t2, t3, own_ref, other_ref, w0, w1, w2, w3, *refs
):
    *biases, msg_ref, back_ref, xk_s, o_s = refs
    col, core = lax.axis_index("col"), lax.axis_index("atom") % NK
    wide = GROUP * TOKS
    packed = (w0, w1, w2, w3)
    t = jnp.concatenate([t0[...], t1[...], t2[...], t3[...]], axis=0)
    xk_s[:, pl.ds(core, 1)] = own_ref[...].reshape(NZ, 1, TOKS, C_S)
    xk_s[:, pl.ds(1 - core, 1)] = other_ref[...].reshape(NZ, 1, TOKS, C_S)
    xk = xk_s[...].reshape(COLS, C_S)
    scores = dot_nt(t, xk)
    groups = [(col + NC - s) % NC for s in range(NC)]
    scores = jnp.concatenate(
        [
            scores[s * wide : (s + 1) * wide]
            + jnp.concatenate(
                [b[pl.ds(groups[s], 1)].reshape(b.shape[1] * GROUP * ROWS, COLS) for b in biases], axis=0
            ).astype(F32)
            for s in range(NC)
        ],
        axis=0,
    )
    top = jnp.max(scores, axis=1, keepdims=True)
    p = jnp.exp(scores - top)
    total = jnp.sum(p, axis=1, keepdims=True)
    mixed = (dot(p.astype(BF), xk) / total).astype(BF)
    blocks = TOKS // ROWS
    lane_head = iota((1, GROUP, 1, GW), 3) // HEAD
    row_head = iota((1, GROUP, 1, GW), 1)
    lane16 = iota((1, GROUP, 1, 128), 3) % H_T
    row16 = iota((1, GROUP, 1, 128), 1)
    tops = jnp.zeros((TOKS, 128), F32)
    totals = jnp.zeros((TOKS, 128), F32)
    for s, w in enumerate(packed):
        lo = s * wide
        o = dot_nt(mixed[lo : lo + wide], w[:GW, :]).reshape(blocks, GROUP, ROWS, GW)
        o = jnp.sum(jnp.where(lane_head == row_head, o, 0.0), axis=1).reshape(TOKS, GW)
        o_s[pl.ds(groups[s], 1)] = o.reshape(1, TOKS, GW)
        folded = jnp.concatenate([w[GW:, i * C_A : (i + 1) * C_A] for i in range(GW // FOLD)], axis=0)
        back_ref.buffer[pl.ds(groups[s], 1)] = folded.reshape(1, GW, C_A)
        here = lane16 == row16 + groups[s] * GROUP
        for value, which in ((top, 0), (total, 1)):
            part = jnp.broadcast_to(value[lo : lo + wide], (wide, 128)).reshape(blocks, GROUP, ROWS, 128)
            part = jnp.sum(jnp.where(here, part, 0.0), axis=1).reshape(TOKS, 128)
            if which == 0:
                tops = tops + part
            else:
                totals = totals + part
    part_of = iota((TOKS, 128), 1) // H_T
    stats = jnp.zeros((TOKS, 128), F32)
    for i, piece in enumerate((*three(tops), *three(totals))):
        stats = jnp.where(part_of == i, piece.astype(F32), stats)
    msg_ref[...] = jnp.concatenate([o_s[g] for g in range(NC)] + [stats], axis=1).astype(BF)


def final_kernel(m0, m1, m2, m3, token_in_ref, state_ref, counts_ref, wback_ref, back_ref, out_ref):
    msgs = [m0[...], m1[...], m2[...], m3[...]]
    r, c = iota((128, 256), 0), iota((128, 256), 1)
    pick = ((r // H_T) // 3 == c // 128) & (r % H_T == c % H_T) & (r < 6 * H_T)
    stats = dot(jnp.concatenate([m[:, C_S:] for m in msgs], axis=0), jnp.where(pick, 1.0, 0.0).astype(BF))
    tops = [stats[i * TOKS : (i + 1) * TOKS, :128] for i in range(NC)]
    totals = [stats[i * TOKS : (i + 1) * TOKS, 128:] for i in range(NC)]
    top = jnp.maximum(jnp.maximum(tops[0], tops[1]), jnp.maximum(tops[2], tops[3]))
    shares = [l * jnp.exp(t - top) for l, t in zip(totals, tops)]
    whole = shares[0] + shares[1] + shares[2] + shares[3]
    r, c = iota((128, C_S), 0), iota((128, C_S), 1)
    expand = jnp.where((r % H_T == c // HEAD) & (r < 2 * H_T), 1.0, 0.0).astype(BF)
    part_of = iota((TOKS, 128), 1) // H_T
    coefs = []
    for share in shares:
        hi, lo = hi_lo(share / whole)
        coefs.append(jnp.where(part_of == 0, hi.astype(F32), lo.astype(F32)).astype(BF))
    scale = dot(jnp.concatenate(coefs, axis=0), expand)
    mix = jnp.zeros((TOKS, C_S), F32)
    for i, m in enumerate(msgs):
        mix = mix + scale[i * TOKS : (i + 1) * TOKS] * m[:, :C_S].astype(F32)
    folded = dot(mix.astype(BF), back_ref[...].reshape(C_S, C_A))
    returned = dot(token_in_ref[...].astype(BF), wback_ref[...]) + folded
    row, _, end_row, _ = spans(counts_ref)
    slots = iota((ATOMS, TOKS), 0).astype(F32)
    onehot = jnp.where((slots < end_row) & (slots >= end_row - row), 1.0, 0.0).astype(BF)
    r_hi, r_lo = hi_lo(returned)
    spread = dot(onehot, r_hi) + dot(onehot, r_lo)
    alive = iota((ATOMS, C_A), 0) < jnp.sum(counts_ref[...], axis=1, keepdims=True)
    out_ref[...] = jnp.where(alive, state_ref[...] + spread, 0.0).astype(BF)


def around(array, axis, size):
    return [lax.ppermute(array, axis, [(i, (i + s) % size) for i in range(size)]) for s in range(1, size)]


def local(
    atom_single, positions, noise_index, token_counts, token_single, pair_repr, w_pos, atom_wq, atom_wk, atom_wv,
    atom_wo, w_pool, trans_w1, trans_w2, w_bias, token_wq, token_wk, token_wv, token_wo, w_back,
):
    atoms = NY * NZ * NK
    counts = token_counts.reshape(1, TOKS)
    initial, normed, inner, outer = call(
        atom_in_kernel,
        [((ATOMS, C_A), F32), ((ATOMS, C_A), BF)] + [((MARGIN, 2 * C_A), BF)] * 2,
        (noise_index, positions, w_pos, atom_single, counts),
        name="atom_in", smem=(0,), flops=1000,
    )
    outer = lax.ppermute(outer, "atom", [(i, i + (1 if i % 2 else -1)) for i in range(1, atoms - 1)])
    inner = lax.ppermute(inner, "atom", [(i, i ^ 1) for i in range(atoms)])
    (packed,) = call(
        pack_kernel, [((GW + FOLD, C_S), BF)], (token_wv.T, token_wo, w_back, normed), name="pack", far=(3,), flops=1000
    )
    weights = [packed] + around(packed, "col", NC)
    pair_out, biases = None, []

    def pair(i, after=None):
        nonlocal pair_out
        pair_out, bias = pair_call(pair_repr, trans_w1, trans_w2, w_bias.T, pair_out, after, *CHUNKS[i])
        biases.append(bias)

    pair(0)
    state, token_in, token_normed, t_own = call(
        atom_mid_kernel,
        [((ATOMS, C_A), F32), ((TOKS, C_S), F32), ((TOKS, C_S), BF), ((GROUP * TOKS, C_S), BF)],
        (
            normed, inner, outer, counts, atom_wq, atom_wk, atom_wv, initial, atom_wo, w_pool, token_single,
            token_wq.T, token_wk.T,
        ),
        name="atom_mid", flops=1000,
    )
    flip = [
        ((y * NZ * NK + i) * NC + x, (x * NZ * NK + i) * NC + y)
        for y in range(NY) for i in range(NZ * NK) for x in range(NC)
    ]
    turned = lax.ppermute(token_normed, ("atom", "col"), flip)
    lines = [[(y * NZ + z) * NK + k for z in range(NZ)] for y in range(NY) for k in range(NK)]
    turned, biases[0], weights = lax.optimization_barrier((turned, biases[0], weights))
    queries = around(t_own, "col", NC)
    own = lax.all_to_all(
        jnp.broadcast_to(turned[None], (NZ, TOKS, C_S)), "atom", 0, 0, axis_index_groups=lines, tiled=True
    )
    pair(1)
    own, biases[1], queries = lax.optimization_barrier((own, biases[1], queries))
    other = lax.ppermute(own, "atom", [(i, i ^ 1) for i in range(atoms)])
    for i in range(2, len(CHUNKS)):
        pair(i)

    msg, back = call(
        attention_kernel,
        [((TOKS, C_S + 128), BF), ((NC, GW, C_A), BF)],
        (t_own, *queries, own, other, *weights, *biases),
        name="attention", flops=1000,
        scratch=[pltpu.VMEM((NZ, NK, TOKS, C_S), BF), pltpu.VMEM((NC, TOKS, GW), F32)],
    )
    msgs = [msg] + around(msg, "col", NC)
    (atom_out,) = call(
        final_kernel, [((ATOMS, C_A), BF)], (*msgs, token_in, state, counts, w_back, back),
        name="final", flops=1000,
    )
    return (atom_out, pair_out)


def solution(mesh):
    placed = (
        P("atom", None), P(None, "atom"), P(), P("atom"), P("atom", None), P("atom", "col", None),
        P(), P(), P(), P(), P(), P(), P(), P(), P(),
        P(None, "col"), P(None, "col"), P(None, "col"), P("col", None), P(),
    )
    return jax.shard_map(
        local,
        mesh=mesh,
        in_specs=placed,
        out_specs=(P("atom", None), P("atom", "col", None)),
        check_vma=False,
    )
```

```python
import math

import jax
import jax.numpy as jnp
from jax import lax
from jax.experimental import pallas as pl
from jax.experimental.pallas import tpu as pltpu
from jax.sharding import PartitionSpec as P

H_A = 4
H_T = 16
WIN_Q = 32
WIN_K = 128
MARGIN = (WIN_K - WIN_Q) // 2
STEPS = 200
EPS = 1e-05
SIGMA_DATA = 16.0
SIGMA_MAX = 160.0
SIGMA_MIN = 0.0004
RHO = 7
MASKED = -1000000000.0

NY = 4
NZ = 8
NK = 2
NC = 4

ATOMS = 512
TOKS = 32
C_A = 128
C_S = 768
GROUP = 4
HEAD = 48
GW = GROUP * HEAD
FOLD = GW * C_A // C_S
ROWS = 8
COLS = 512
CHUNKS = ((0, 1), (1, 3))

F32 = jnp.float32
BF = jnp.bfloat16


def dot(a, b):
    return jnp.dot(a, b, preferred_element_type=F32)


def dot_nt(a, b):
    return lax.dot_general(a, b, (((1,), (1,)), ((), ())), preferred_element_type=F32)


def iota(shape, dim):
    return lax.broadcasted_iota(jnp.int32, shape, dim)


def hi_lo(v):
    hi = v.astype(BF)
    return hi, (v - hi.astype(F32)).astype(BF)


def three(v):
    hi = v.astype(BF)
    rest = v - hi.astype(F32)
    mid = rest.astype(BF)
    return hi, mid, (rest - mid.astype(F32)).astype(BF)


def normalize(values):
    average = jnp.mean(values, axis=-1, keepdims=True)
    centred = values - average
    variance = jnp.mean(centred * centred, axis=-1, keepdims=True)
    return centred * lax.rsqrt(variance + EPS)


class Fetched:
    def __init__(self, copy, buffer):
        self.copy, self.buffer, self.here, self.shape = copy, buffer, False, buffer.shape

    def arrive(self):
        if not self.here:
            self.copy.wait()
            self.here = True

    def __getitem__(self, index):
        self.arrive()
        return self.buffer[index]


class Sent:
    def __init__(self, copy, buffer):
        self.copy, self.buffer, self.gone = copy, buffer, False

    def __setitem__(self, index, value):
        self.buffer[index] = value

    def send(self):
        if not self.gone:
            self.copy.start()
            self.gone = True


def call(kernel, outs, args, *, name, smem=(), scratch=(), far=(), aliases=None, flops=0):
    n, m, k = len(args), len(outs), len(scratch)
    fetch = [i for i in range(n) if i not in smem and i not in far]
    send = [i for i in range(m) if n + i not in far]

    def body(*refs):
        ins, given, rest = list(refs[:n]), list(refs[n : n + m]), refs[n + m : n + m + k]
        buffers, sems = refs[n + m + k : -1], refs[-1]
        for slot, i in enumerate(fetch):
            copy = pltpu.make_async_copy(ins[i], buffers[slot], sems.at[slot])
            copy.start()
            ins[i] = Fetched(copy, buffers[slot])
        for slot, i in enumerate(send, len(fetch)):
            given[i] = Sent(pltpu.make_async_copy(buffers[slot], given[i], sems.at[slot]), buffers[slot])
        kernel(*ins, *given, *rest)
        for i in fetch:
            ins[i].arrive()
        for i in send:
            given[i].send()
        for i in send:
            given[i].copy.wait()

    return pl.pallas_call(
        body,
        in_specs=[pl.BlockSpec(memory_space=pltpu.SMEM if i in smem else pltpu.HBM) for i in range(n)],
        out_specs=[pl.BlockSpec(memory_space=pltpu.HBM)] * m,
        out_shape=[jax.ShapeDtypeStruct(s, d) for s, d in outs],
        scratch_shapes=[
            *scratch,
            *(pltpu.VMEM(args[i].shape, args[i].dtype) for i in fetch),
            *(pltpu.VMEM(*outs[i]) for i in send),
            pltpu.SemaphoreType.DMA((max(len(fetch) + len(send), 1),)),
        ],
        input_output_aliases=aliases or {},
        compiler_params=pltpu.CompilerParams(vmem_limit_bytes=56 * 2**20),
        cost_estimate=pl.CostEstimate(flops=flops, bytes_accessed=1024, transcendentals=0),
        name=name,
    )(*args)


def atom_in_kernel(
    noise_ref, pos_ref, wpos_ref, single_ref, counts_ref, initial_ref, normed_ref, inner_ref, outer_ref
):
    level = jnp.full((1, C_A), noise_ref[0], jnp.int32).astype(F32)
    upper = SIGMA_MAX ** (1.0 / RHO)
    lower = SIGMA_MIN ** (1.0 / RHO)
    root = upper + level / (STEPS - 1) * (lower - upper)
    square = root * root
    sigma = square * square * square * root
    gain = 1.0 / jnp.sqrt(sigma * sigma + SIGMA_DATA * SIGMA_DATA)
    lifted = lax.dot_general(
        pos_ref[...], wpos_ref[...] * gain, (((0,), (0,)), ((), ())),
        precision=lax.Precision.HIGHEST, preferred_element_type=F32,
    )
    initial = single_ref[...].astype(F32) + lifted
    normed = normalize(initial).astype(BF)
    total = jnp.sum(counts_ref[...], axis=1, keepdims=True)
    slots = iota((ATOMS, C_A), 0)
    live = jnp.where(slots < total, 1.0, 0.0).astype(BF)
    both = jnp.concatenate([normed, live], axis=1)
    first, last = both[:MARGIN].astype(F32), both[ATOMS - MARGIN :].astype(F32)
    lower = lax.axis_index("atom") % NK == 0
    inner_ref[...] = jnp.where(lower, last, first).astype(BF)
    inner_ref.send()
    outer_ref[...] = jnp.where(lower, first, last).astype(BF)
    outer_ref.send()
    normed_ref[...] = normed
    normed_ref.send()
    initial_ref[...] = initial


def spans(counts_ref):
    row = counts_ref[...].astype(F32)
    grid = jnp.broadcast_to(row, (TOKS, TOKS))
    r, c = iota((TOKS, TOKS), 0), iota((TOKS, TOKS), 1)
    count_col = jnp.sum(jnp.where(r == c, grid, 0.0), axis=1, keepdims=True)
    end_col = jnp.sum(jnp.where(c <= r, grid, 0.0), axis=1, keepdims=True)
    end_row = jnp.sum(jnp.where(r <= c, jnp.broadcast_to(count_col, (TOKS, TOKS)), 0.0), axis=0, keepdims=True)
    return row, count_col, end_row, end_col


def atom_mid_kernel(
    normed_ref, inner_ref, outer_ref, counts_ref, wq_ref, wk_ref, wv_ref, initial_ref, wo_ref, pool_ref,
    single_ref, twq_ref, twk_ref, twv_ref, two_ref, back_ref, state_ref, token_in_ref, token_normed_ref, t_ref,
):
    lower = lax.axis_index("atom") % NK == 0
    inner, outer = inner_ref[...].astype(F32), outer_ref[...].astype(F32)
    before = jnp.where(lower, outer, inner).astype(BF)
    after = jnp.where(lower, inner, outer).astype(BF)
    normed = normed_ref[...]
    _, count_col, _, end_col = spans(counts_ref)
    slots = iota((TOKS, ATOMS), 1).astype(F32)
    onehot = jnp.where((slots < end_col) & (slots >= end_col - count_col), 1.0, 0.0).astype(BF)
    wide = jnp.concatenate([before[:, :C_A], normed, after[:, :C_A]], axis=0)
    n_before = jnp.sum(before[:, C_A:].astype(F32), axis=0, keepdims=True)
    n_after = jnp.sum(after[:, C_A:].astype(F32), axis=0, keepdims=True)
    n_own = jnp.sum(counts_ref[...].astype(F32), axis=1, keepdims=True)
    queries = dot(normed, wq_ref[...]).astype(BF)
    keys = dot(wide, wk_ref[...]).astype(BF)
    values = dot(wide, wv_ref[...]).astype(BF)
    stacked = H_A * WIN_Q
    mine = iota((stacked, C_A), 1) // (C_A // H_A) == iota((stacked, C_A), 0) // WIN_Q
    pick = jnp.where(mine, 1.0, 0.0).astype(BF)
    scale = 1.0 / math.sqrt(C_A // H_A)
    windows = ATOMS // WIN_Q
    scores = []
    for w in range(windows):
        q = queries[w * WIN_Q : (w + 1) * WIN_Q]
        q4 = jnp.concatenate([q] * H_A, axis=0) * pick
        slot = (iota((1, WIN_K), 1) + (w * WIN_Q - MARGIN)).astype(F32)
        bound = jnp.broadcast_to(n_own, (1, WIN_K))
        if w * WIN_Q < MARGIN:
            bound = jnp.where(slot < 0, n_before - MARGIN, bound)
        if w * WIN_Q - MARGIN + WIN_K > ATOMS:
            bound = jnp.where(slot >= ATOMS, n_after + ATOMS, bound)
        penalty = jnp.where(slot < bound, 0.0, MASKED)
        scores.append(dot_nt(q4, keys[w * WIN_Q : w * WIN_Q + WIN_K]) * scale + penalty)
    scores = jnp.concatenate(scores, axis=0)
    p = jnp.exp(scores - jnp.max(scores, axis=1, keepdims=True))
    weight = (p / jnp.sum(p, axis=1, keepdims=True)).astype(BF)
    mixes = []
    for w in range(windows):
        o = dot(weight[w * stacked : (w + 1) * stacked], values[w * WIN_Q : w * WIN_Q + WIN_K])
        o = jnp.where(mine, o, 0.0)
        mixes.append(o[:32] + o[32:64] + o[64:96] + o[96:])
    mix = jnp.concatenate(mixes, axis=0).astype(BF)
    state = initial_ref[...] + dot(mix, wo_ref[...])
    state_ref[...] = state
    state_ref.send()
    features = jnp.maximum(dot(state.astype(BF), pool_ref[...]), 0.0)
    f_hi, f_lo = hi_lo(features)
    sums = dot(onehot, f_hi) + dot(onehot, f_lo)
    token_in = single_ref[...].astype(F32) + sums / count_col
    token_normed = normalize(token_in).astype(BF)
    token_normed_ref[...] = token_normed
    token_normed_ref.send()
    token_in_ref[...] = token_in
    token_in_ref.send()
    tq = dot_nt(token_normed, twq_ref[...]).astype(BF).astype(F32)
    lanes = iota((ROWS, GW), 1) // HEAD
    pieces = [
        jnp.where(lanes == h, tq[ib * ROWS : (ib + 1) * ROWS], 0.0)
        for ib in range(TOKS // ROWS)
        for h in range(GROUP)
    ]
    spread = jnp.concatenate(pieces, axis=0).astype(BF)
    t_ref[: GROUP * TOKS, :] = (dot(spread, twk_ref[...]) * (1.0 / math.sqrt(HEAD))).astype(BF)
    t_ref[GROUP * TOKS : GROUP * TOKS + GW, :] = twv_ref[...]
    folded = dot(two_ref[...], back_ref[...]).astype(BF)
    t_ref[GROUP * TOKS + GW :, :] = jnp.concatenate(
        [folded[i * FOLD : (i + 1) * FOLD] for i in range(GW // FOLD)], axis=1
    )


def pair_kernel(x_ref, w1_ref, w2_ref, wb_ref, *refs, start, count):
    out_ref, bias_ref, x_s, y_s, b_s, w1_s, w2_s, in_sem, out_sem, bias_sem = refs[-10:]
    pairs = ROWS // 2
    arrivals = [
        pltpu.make_async_copy(x_ref.at[pl.ds((start + i) * ROWS, ROWS)], x_s.at[i], in_sem.at[i])
        for i in range(count)
    ]
    leaving = [
        pltpu.make_async_copy(
            y_s.at[i, pl.ds(k * pairs, pairs)],
            out_ref.at[pl.ds((start + i) * ROWS + k * pairs, pairs)],
            out_sem.at[2 * i + k],
        )
        for i in range(count)
        for k in range(2)
    ]
    biases = [
        pltpu.make_async_copy(b_s.at[:, i], bias_ref.at[:, i], bias_sem.at[i]) for i in range(count)
    ]
    for copy in arrivals:
        copy.start()
    r, c = iota((256, 256), 0), iota((256, 256), 1)
    same = (r // 128) == (c // 128)
    centre = (jnp.where(r == c, 1.0, 0.0) - jnp.where(same, 1.0 / 128, 0.0)).astype(BF)
    w1_s[:, :256] = w1_ref[:, :256] * jnp.asarray(0.5, BF)
    w1_s[:, 256:] = w1_ref[:, 256:]
    w2 = w2_ref[...]
    w2_s[:, :128] = w2
    wide = w2.astype(F32)
    w2_s[:, 128:] = (wide - jnp.mean(wide, axis=1, keepdims=True)).astype(BF)
    head, lane = iota((H_T, 128), 0), iota((H_T, 128), 1)
    wb = wb_ref[...]
    heads = [
        lax.dot_general(
            wb, jnp.where(lane == head * ROWS + g, 1.0, 0.0).astype(BF), (((0,), (0,)), ((), ())),
            preferred_element_type=F32,
        ).astype(BF)
        for g in range(ROWS)
    ]
    heads = [jnp.concatenate([heads[p], heads[pairs + p]], axis=0) for p in range(pairs)]
    m = pairs * COLS
    for step in range(count):
        arrivals[step].wait()
        xs = [x_s[step, :pairs].reshape(m, 128), x_s[step, pairs:].reshape(m, 128)]
        c = dot(jnp.concatenate(xs, axis=1), centre)
        kept = []
        for k in range(2):
            ck = c[:, 128 * k : 128 * k + 128]
            n = (ck * lax.rsqrt(jnp.mean(ck * ck, axis=1, keepdims=True) + EPS)).astype(BF)
            g = dot(n, w1_s[...])
            gate, up = g[:, :256], g[:, 256:]
            h = ((gate + gate * jnp.tanh(gate)) * up).astype(BF)
            u = dot(h, w2_s[...])
            y_s[step, k * pairs : (k + 1) * pairs] = (
                (xs[k].astype(F32) + u[:, :128]).astype(BF).reshape(pairs, COLS, 128)
            )
            c2 = ck + u[:, 128:]
            kept.append((c2 * lax.rsqrt(jnp.mean(c2 * c2, axis=1, keepdims=True) + EPS)).astype(BF))
            leaving[2 * step + k].start()
        cc = jnp.concatenate(kept, axis=1)
        acc = jnp.zeros((COLS, 128), F32)
        for p in range(pairs):
            acc = acc + dot(cc[p * COLS : (p + 1) * COLS], heads[p])
        b_s[:, step] = acc.T.astype(BF).reshape(NC, GROUP * ROWS, COLS)
        biases[step].start()
    for copy in (*leaving, *biases):
        copy.wait()


def pair_call(x, w1, w2, wb, prior, after, start, count):
    block = (count, ROWS, COLS, 128)
    more = [a for a in (prior, after) if a is not None]
    n = 4 + len(more)
    return call(
        lambda *refs: pair_kernel(*refs, start=start, count=count),
        [(x.shape, BF), ((NC, count, GROUP * ROWS, COLS), BF)],
        (x, w1, w2, wb, *more),
        name="pair", far=(0, *range(4, n + 2)), aliases={} if prior is None else {4: 0},
        scratch=[
            pltpu.VMEM(block, BF), pltpu.VMEM(block, BF), pltpu.VMEM((NC, count, GROUP * ROWS, COLS), BF),
            pltpu.VMEM((128, 512), BF), pltpu.VMEM((256, 256), BF),
            *(pltpu.SemaphoreType.DMA((i * count,)) for i in (1, 2, 1)),
        ],
        flops=count * 3 * 10**9,
    )


def attention_kernel(
    t0, t1, t2, t3, own_ref, other_ref, *refs
):
    *biases, msg_ref, back_ref, xk_s, o_s = refs
    col, core = lax.axis_index("col"), lax.axis_index("atom") % NK
    xk_s[:, pl.ds(core, 1)] = own_ref[...].reshape(NZ, 1, TOKS, C_S)
    xk_s[:, pl.ds(1 - core, 1)] = other_ref[...].reshape(NZ, 1, TOKS, C_S)
    xk = xk_s[...].reshape(COLS, C_S)
    wide = GROUP * TOKS
    packed = (t0, t1, t2, t3)
    t = jnp.concatenate([p[:wide, :] for p in packed], axis=0)
    scores = dot_nt(t, xk)
    groups = [(col + NC - s) % NC for s in range(NC)]
    scores = jnp.concatenate(
        [
            scores[s * wide : (s + 1) * wide]
            + jnp.concatenate(
                [b[pl.ds(groups[s], 1)].reshape(b.shape[1] * GROUP * ROWS, COLS) for b in biases], axis=0
            ).astype(F32)
            for s in range(NC)
        ],
        axis=0,
    )
    top = jnp.max(scores, axis=1, keepdims=True)
    p = jnp.exp(scores - top)
    total = jnp.sum(p, axis=1, keepdims=True)
    mixed = (dot(p.astype(BF), xk) / total).astype(BF)
    blocks = TOKS // ROWS
    lane_head = iota((1, GROUP, 1, GW), 3) // HEAD
    row_head = iota((1, GROUP, 1, GW), 1)
    lane16 = iota((1, GROUP, 1, 128), 3) % H_T
    row16 = iota((1, GROUP, 1, 128), 1)
    tops = jnp.zeros((TOKS, 128), F32)
    totals = jnp.zeros((TOKS, 128), F32)
    for s, w in enumerate(packed):
        lo = s * wide
        o = dot_nt(mixed[lo : lo + wide], w[wide : wide + GW, :]).reshape(blocks, GROUP, ROWS, GW)
        o = jnp.sum(jnp.where(lane_head == row_head, o, 0.0), axis=1).reshape(TOKS, GW)
        o_s[pl.ds(groups[s], 1)] = o.reshape(1, TOKS, GW)
        folded = jnp.concatenate([w[wide + GW :, i * C_A : (i + 1) * C_A] for i in range(GW // FOLD)], axis=0)
        back_ref.buffer[pl.ds(groups[s], 1)] = folded.reshape(1, GW, C_A)
        here = lane16 == row16 + groups[s] * GROUP
        for value, which in ((top, 0), (total, 1)):
            part = jnp.broadcast_to(value[lo : lo + wide], (wide, 128)).reshape(blocks, GROUP, ROWS, 128)
            part = jnp.sum(jnp.where(here, part, 0.0), axis=1).reshape(TOKS, 128)
            if which == 0:
                tops = tops + part
            else:
                totals = totals + part
    part_of = iota((TOKS, 128), 1) // H_T
    stats = jnp.zeros((TOKS, 128), F32)
    for i, piece in enumerate((*three(tops), *three(totals))):
        stats = jnp.where(part_of == i, piece.astype(F32), stats)
    msg_ref[...] = jnp.concatenate([o_s[g] for g in range(NC)] + [stats], axis=1).astype(BF)


def final_kernel(m0, m1, m2, m3, token_in_ref, state_ref, counts_ref, wback_ref, back_ref, out_ref):
    msgs = [m0[...], m1[...], m2[...], m3[...]]
    r, c = iota((128, 256), 0), iota((128, 256), 1)
    pick = ((r // H_T) // 3 == c // 128) & (r % H_T == c % H_T) & (r < 6 * H_T)
    stats = dot(jnp.concatenate([m[:, C_S:] for m in msgs], axis=0), jnp.where(pick, 1.0, 0.0).astype(BF))
    tops = [stats[i * TOKS : (i + 1) * TOKS, :128] for i in range(NC)]
    totals = [stats[i * TOKS : (i + 1) * TOKS, 128:] for i in range(NC)]
    top = jnp.maximum(jnp.maximum(tops[0], tops[1]), jnp.maximum(tops[2], tops[3]))
    shares = [l * jnp.exp(t - top) for l, t in zip(totals, tops)]
    whole = shares[0] + shares[1] + shares[2] + shares[3]
    r, c = iota((128, C_S), 0), iota((128, C_S), 1)
    expand = jnp.where((r % H_T == c // HEAD) & (r < 2 * H_T), 1.0, 0.0).astype(BF)
    part_of = iota((TOKS, 128), 1) // H_T
    coefs = []
    for share in shares:
        hi, lo = hi_lo(share / whole)
        coefs.append(jnp.where(part_of == 0, hi.astype(F32), lo.astype(F32)).astype(BF))
    scale = dot(jnp.concatenate(coefs, axis=0), expand)
    mix = jnp.zeros((TOKS, C_S), F32)
    for i, m in enumerate(msgs):
        mix = mix + scale[i * TOKS : (i + 1) * TOKS] * m[:, :C_S].astype(F32)
    folded = dot(mix.astype(BF), back_ref[...].reshape(C_S, C_A))
    returned = dot(token_in_ref[...].astype(BF), wback_ref[...]) + folded
    row, _, end_row, _ = spans(counts_ref)
    slots = iota((ATOMS, TOKS), 0).astype(F32)
    onehot = jnp.where((slots < end_row) & (slots >= end_row - row), 1.0, 0.0).astype(BF)
    r_hi, r_lo = hi_lo(returned)
    spread = dot(onehot, r_hi) + dot(onehot, r_lo)
    alive = iota((ATOMS, C_A), 0) < jnp.sum(counts_ref[...], axis=1, keepdims=True)
    out_ref[...] = jnp.where(alive, state_ref[...] + spread, 0.0).astype(BF)


def around(array, axis, size):
    return [lax.ppermute(array, axis, [(i, (i + s) % size) for i in range(size)]) for s in range(1, size)]


def local(
    atom_single, positions, noise_index, token_counts, token_single, pair_repr, w_pos, atom_wq, atom_wk, atom_wv,
    atom_wo, w_pool, trans_w1, trans_w2, w_bias, token_wq, token_wk, token_wv, token_wo, w_back,
):
    atoms = NY * NZ * NK
    counts = token_counts.reshape(1, TOKS)
    initial, normed, inner, outer = call(
        atom_in_kernel,
        [((ATOMS, C_A), F32), ((ATOMS, C_A), BF), ((MARGIN, 2 * C_A), BF), ((MARGIN, 2 * C_A), BF)],
        (noise_index, positions, w_pos, atom_single, counts),
        name="atom_in", smem=(0,), flops=10**8,
    )
    outer = lax.ppermute(outer, "atom", [(i, i + (1 if i % 2 else -1)) for i in range(1, atoms - 1)])
    inner = lax.ppermute(inner, "atom", [(i, i ^ 1) for i in range(atoms)])
    pair_out, biases = None, []

    def pair(i, after=None):
        nonlocal pair_out
        pair_out, bias = pair_call(pair_repr, trans_w1, trans_w2, w_bias.T, pair_out, after, *CHUNKS[i])
        biases.append(bias)

    pair(0)
    state, token_in, token_normed, t_own = call(
        atom_mid_kernel,
        [((ATOMS, C_A), F32), ((TOKS, C_S), F32), ((TOKS, C_S), BF), ((GROUP * TOKS + GW + FOLD, C_S), BF)],
        (
            normed, inner, outer, counts, atom_wq, atom_wk, atom_wv, initial, atom_wo, w_pool, token_single,
            token_wq.T, token_wk.T, token_wv.T, token_wo, w_back,
        ),
        name="atom_mid", flops=10**9,
    )
    flip = [
        ((y * NZ * NK + i) * NC + x, (x * NZ * NK + i) * NC + y)
        for y in range(NY) for i in range(NZ * NK) for x in range(NC)
    ]
    turned = lax.ppermute(token_normed, ("atom", "col"), flip)
    lines = [[(y * NZ + z) * NK + k for z in range(NZ)] for y in range(NY) for k in range(NK)]
    turned, biases[0], t_own = lax.optimization_barrier((turned, biases[0], t_own))
    own = lax.all_to_all(
        jnp.broadcast_to(turned[None], (NZ, TOKS, C_S)), "atom", 0, 0, axis_index_groups=lines, tiled=True
    )
    one = lax.ppermute(t_own, "col", [(i, (i + 1) % NC) for i in range(NC)])
    three_on = lax.ppermute(t_own, "col", [(i, (i - 1) % NC) for i in range(NC)])
    two = lax.ppermute(one, "col", [(i, (i + 1) % NC) for i in range(NC)])
    pair(1)
    packed = [t_own, one, two, three_on]
    own, biases[1], packed = lax.optimization_barrier((own, biases[1], packed))
    other = lax.ppermute(own, "atom", [(i, i ^ 1) for i in range(atoms)])
    for i in range(2, len(CHUNKS)):
        pair(i)

    msg, back = call(
        attention_kernel,
        [((TOKS, C_S + 128), BF), ((NC, GW, C_A), BF)],
        (*packed, own, other, *biases),
        name="attention", flops=3 * 10**9,
        scratch=[pltpu.VMEM((NZ, NK, TOKS, C_S), BF), pltpu.VMEM((NC, TOKS, GW), F32)],
    )
    msgs = [msg] + around(msg, "col", NC)
    (atom_out,) = call(
        final_kernel, [((ATOMS, C_A), BF)], (*msgs, token_in, state, counts, w_back, back),
        name="final", flops=10**8,
    )
    return (atom_out, pair_out)


def solution(mesh):
    placed = (
        P("atom", None), P(None, "atom"), P(), P("atom"), P("atom", None), P("atom", "col", None),
        P(), P(), P(), P(), P(), P(), P(), P(), P(),
        P(None, "col"), P(None, "col"), P(None, "col"), P("col", None), P(),
    )
    return jax.shard_map(
        local,
        mesh=mesh,
        in_specs=placed,
        out_specs=(P("atom", None), P("atom", "col", None)),
        check_vma=False,
    )
```

```python
import math

import jax
import jax.numpy as jnp
from jax import lax
from jax.experimental import pallas as pl
from jax.experimental.pallas import tpu as pltpu
from jax.sharding import PartitionSpec as P

H_A = 4
H_T = 16
WIN_Q = 32
WIN_K = 128
MARGIN = (WIN_K - WIN_Q) // 2
STEPS = 200
EPS = 1e-05
SIGMA_DATA = 16.0
SIGMA_MAX = 160.0
SIGMA_MIN = 0.0004
RHO = 7
MASKED = -1000000000.0

NY = 4
NZ = 8
NK = 2
NC = 4

ATOMS = 512
TOKS = 32
C_A = 128
C_S = 768
GROUP = 4
HEAD = 48
GW = GROUP * HEAD
FOLD = GW * C_A // C_S
ROWS = 8
COLS = 512
CHUNKS = ((0, 1), (1, 3))

F32 = jnp.float32
BF = jnp.bfloat16


def dot(a, b):
    return jnp.dot(a, b, preferred_element_type=F32)


def dot_nt(a, b):
    return lax.dot_general(a, b, (((1,), (1,)), ((), ())), preferred_element_type=F32)


def iota(shape, dim):
    return lax.broadcasted_iota(jnp.int32, shape, dim)


def hi_lo(v):
    hi = v.astype(BF)
    return hi, (v - hi.astype(F32)).astype(BF)


def three(v):
    hi = v.astype(BF)
    rest = v - hi.astype(F32)
    mid = rest.astype(BF)
    return hi, mid, (rest - mid.astype(F32)).astype(BF)


def normalize(values):
    average = jnp.mean(values, axis=-1, keepdims=True)
    centred = values - average
    variance = jnp.mean(centred * centred, axis=-1, keepdims=True)
    return centred * lax.rsqrt(variance + EPS)


class Fetched:
    def __init__(self, copy, buffer):
        self.copy, self.buffer, self.here, self.shape = copy, buffer, False, buffer.shape

    def arrive(self):
        if not self.here:
            self.copy.wait()
            self.here = True

    def __getitem__(self, index):
        self.arrive()
        return self.buffer[index]


class Sent:
    def __init__(self, copy, buffer):
        self.copy, self.buffer, self.gone = copy, buffer, False

    def __setitem__(self, index, value):
        self.buffer[index] = value

    def send(self):
        if not self.gone:
            self.copy.start()
            self.gone = True


def call(kernel, outs, args, *, name, smem=(), scratch=(), far=(), aliases=None, flops=0):
    n, m, k = len(args), len(outs), len(scratch)
    fetch = [i for i in range(n) if i not in smem and i not in far]
    send = [i for i in range(m) if n + i not in far]

    def body(*refs):
        ins, given, rest = list(refs[:n]), list(refs[n : n + m]), refs[n + m : n + m + k]
        buffers, sems = refs[n + m + k : -1], refs[-1]
        for slot, i in enumerate(fetch):
            copy = pltpu.make_async_copy(ins[i], buffers[slot], sems.at[slot])
            copy.start()
            ins[i] = Fetched(copy, buffers[slot])
        for slot, i in enumerate(send, len(fetch)):
            given[i] = Sent(pltpu.make_async_copy(buffers[slot], given[i], sems.at[slot]), buffers[slot])
        kernel(*ins, *given, *rest)
        for i in fetch:
            ins[i].arrive()
        for i in send:
            given[i].send()
        for i in send:
            given[i].copy.wait()

    return pl.pallas_call(
        body,
        in_specs=[pl.BlockSpec(memory_space=pltpu.SMEM if i in smem else pltpu.HBM) for i in range(n)],
        out_specs=[pl.BlockSpec(memory_space=pltpu.HBM)] * m,
        out_shape=[jax.ShapeDtypeStruct(s, d) for s, d in outs],
        scratch_shapes=[
            *scratch,
            *(pltpu.VMEM(args[i].shape, args[i].dtype) for i in fetch),
            *(pltpu.VMEM(*outs[i]) for i in send),
            pltpu.SemaphoreType.DMA((max(len(fetch) + len(send), 1),)),
        ],
        input_output_aliases=aliases or {},
        compiler_params=pltpu.CompilerParams(vmem_limit_bytes=56 * 2**20),
        cost_estimate=pl.CostEstimate(flops=flops, bytes_accessed=1024, transcendentals=0),
        name=name,
    )(*args)


def atom_in_kernel(
    noise_ref, pos_ref, wpos_ref, single_ref, counts_ref, initial_ref, normed_ref, inner_ref, outer_ref
):
    level = jnp.full((1, C_A), noise_ref[0], jnp.int32).astype(F32)
    upper = SIGMA_MAX ** (1.0 / RHO)
    lower = SIGMA_MIN ** (1.0 / RHO)
    root = upper + level / (STEPS - 1) * (lower - upper)
    square = root * root
    sigma = square * square * square * root
    gain = 1.0 / jnp.sqrt(sigma * sigma + SIGMA_DATA * SIGMA_DATA)
    lifted = lax.dot_general(
        pos_ref[...], wpos_ref[...] * gain, (((0,), (0,)), ((), ())),
        precision=lax.Precision.HIGHEST, preferred_element_type=F32,
    )
    initial = single_ref[...].astype(F32) + lifted
    normed = normalize(initial).astype(BF)
    total = jnp.sum(counts_ref[...], axis=1, keepdims=True)
    slots = iota((ATOMS, C_A), 0)
    live = jnp.where(slots < total, 1.0, 0.0).astype(BF)
    both = jnp.concatenate([normed, live], axis=1)
    first, last = both[:MARGIN].astype(F32), both[ATOMS - MARGIN :].astype(F32)
    lower = lax.axis_index("atom") % NK == 0
    inner_ref[...] = jnp.where(lower, last, first).astype(BF)
    inner_ref.send()
    outer_ref[...] = jnp.where(lower, first, last).astype(BF)
    outer_ref.send()
    normed_ref[...] = normed
    normed_ref.send()
    initial_ref[...] = initial


def spans(counts_ref):
    row = counts_ref[...].astype(F32)
    grid = jnp.broadcast_to(row, (TOKS, TOKS))
    r, c = iota((TOKS, TOKS), 0), iota((TOKS, TOKS), 1)
    count_col = jnp.sum(jnp.where(r == c, grid, 0.0), axis=1, keepdims=True)
    end_col = jnp.sum(jnp.where(c <= r, grid, 0.0), axis=1, keepdims=True)
    end_row = jnp.sum(jnp.where(r <= c, jnp.broadcast_to(count_col, (TOKS, TOKS)), 0.0), axis=0, keepdims=True)
    return row, count_col, end_row, end_col


def atom_mid_kernel(
    normed_ref, inner_ref, outer_ref, counts_ref, wq_ref, wk_ref, wv_ref, initial_ref, wo_ref, pool_ref,
    single_ref, twq_ref, twk_ref, twv_ref, two_ref, back_ref, state_ref, token_in_ref, token_normed_ref, t_ref,
):
    lower = lax.axis_index("atom") % NK == 0
    inner, outer = inner_ref[...].astype(F32), outer_ref[...].astype(F32)
    before = jnp.where(lower, outer, inner).astype(BF)
    after = jnp.where(lower, inner, outer).astype(BF)
    normed = normed_ref[...]
    _, count_col, _, end_col = spans(counts_ref)
    slots = iota((TOKS, ATOMS), 1).astype(F32)
    onehot = jnp.where((slots < end_col) & (slots >= end_col - count_col), 1.0, 0.0).astype(BF)
    wide = jnp.concatenate([before[:, :C_A], normed, after[:, :C_A]], axis=0)
    n_before = jnp.sum(before[:, C_A:].astype(F32), axis=0, keepdims=True)
    n_after = jnp.sum(after[:, C_A:].astype(F32), axis=0, keepdims=True)
    n_own = jnp.sum(counts_ref[...].astype(F32), axis=1, keepdims=True)
    queries = dot(normed, wq_ref[...]).astype(BF)
    keys = dot(wide, wk_ref[...]).astype(BF)
    values = dot(wide, wv_ref[...]).astype(BF)
    stacked = H_A * WIN_Q
    mine = iota((stacked, C_A), 1) // (C_A // H_A) == iota((stacked, C_A), 0) // WIN_Q
    pick = jnp.where(mine, 1.0, 0.0).astype(BF)
    scale = 1.0 / math.sqrt(C_A // H_A)
    windows = ATOMS // WIN_Q
    scores = []
    for w in range(windows):
        q = queries[w * WIN_Q : (w + 1) * WIN_Q]
        q4 = jnp.concatenate([q] * H_A, axis=0) * pick
        slot = (iota((1, WIN_K), 1) + (w * WIN_Q - MARGIN)).astype(F32)
        bound = jnp.broadcast_to(n_own, (1, WIN_K))
        if w * WIN_Q < MARGIN:
            bound = jnp.where(slot < 0, n_before - MARGIN, bound)
        if w * WIN_Q - MARGIN + WIN_K > ATOMS:
            bound = jnp.where(slot >= ATOMS, n_after + ATOMS, bound)
        penalty = jnp.where(slot < bound, 0.0, MASKED)
        scores.append(dot_nt(q4, keys[w * WIN_Q : w * WIN_Q + WIN_K]) * scale + penalty)
    scores = jnp.concatenate(scores, axis=0)
    p = jnp.exp(scores - jnp.max(scores, axis=1, keepdims=True))
    weight = (p / jnp.sum(p, axis=1, keepdims=True)).astype(BF)
    mixes = []
    for w in range(windows):
        o = dot(weight[w * stacked : (w + 1) * stacked], values[w * WIN_Q : w * WIN_Q + WIN_K])
        o = jnp.where(mine, o, 0.0)
        mixes.append(o[:32] + o[32:64] + o[64:96] + o[96:])
    mix = jnp.concatenate(mixes, axis=0).astype(BF)
    state = initial_ref[...] + dot(mix, wo_ref[...])
    state_ref[...] = state
    state_ref.send()
    features = jnp.maximum(dot(state.astype(BF), pool_ref[...]), 0.0)
    f_hi, f_lo = hi_lo(features)
    sums = dot(onehot, f_hi) + dot(onehot, f_lo)
    token_in = single_ref[...].astype(F32) + sums / count_col
    token_normed = normalize(token_in).astype(BF)
    token_normed_ref[...] = token_normed
    token_normed_ref.send()
    token_in_ref[...] = token_in
    token_in_ref.send()
    tq = dot_nt(token_normed, twq_ref[...]).astype(BF).astype(F32)
    lanes = iota((ROWS, GW), 1) // HEAD
    pieces = [
        jnp.where(lanes == h, tq[ib * ROWS : (ib + 1) * ROWS], 0.0)
        for ib in range(TOKS // ROWS)
        for h in range(GROUP)
    ]
    spread = jnp.concatenate(pieces, axis=0).astype(BF)
    t_ref[: GROUP * TOKS, :] = (dot(spread, twk_ref[...]) * (1.0 / math.sqrt(HEAD))).astype(BF)
    t_ref[GROUP * TOKS : GROUP * TOKS + GW, :] = twv_ref[...]
    folded = dot(two_ref[...], back_ref[...]).astype(BF)
    t_ref[GROUP * TOKS + GW :, :] = jnp.concatenate(
        [folded[i * FOLD : (i + 1) * FOLD] for i in range(GW // FOLD)], axis=1
    )


def pair_kernel(x_ref, w1_ref, w2_ref, wb_ref, *refs, start, count):
    out_ref, bias_ref, x_s, y_s, b_s, w1_s, w2_s, in_sem, out_sem, bias_sem = refs[-10:]
    pairs = ROWS // 2
    arrivals = [
        pltpu.make_async_copy(x_ref.at[pl.ds((start + i) * ROWS, ROWS)], x_s.at[i], in_sem.at[i])
        for i in range(count)
    ]
    leaving = [
        pltpu.make_async_copy(
            y_s.at[i, pl.ds(k * pairs, pairs)],
            out_ref.at[pl.ds((start + i) * ROWS + k * pairs, pairs)],
            out_sem.at[2 * i + k],
        )
        for i in range(count)
        for k in range(2)
    ]
    biases = [
        pltpu.make_async_copy(b_s.at[:, i], bias_ref.at[:, i], bias_sem.at[i]) for i in range(count)
    ]
    for copy in arrivals:
        copy.start()
    r, c = iota((256, 256), 0), iota((256, 256), 1)
    same = (r // 128) == (c // 128)
    centre = (jnp.where(r == c, 1.0, 0.0) - jnp.where(same, 1.0 / 128, 0.0)).astype(BF)
    w1_s[:, :256] = w1_ref[:, :256] * jnp.asarray(0.5, BF)
    w1_s[:, 256:] = w1_ref[:, 256:]
    w2 = w2_ref[...]
    w2_s[:, :128] = w2
    wide = w2.astype(F32)
    w2_s[:, 128:] = (wide - jnp.mean(wide, axis=1, keepdims=True)).astype(BF)
    head, lane = iota((H_T, 128), 0), iota((H_T, 128), 1)
    wb = wb_ref[...]
    heads = [
        lax.dot_general(
            wb, jnp.where(lane == head * ROWS + g, 1.0, 0.0).astype(BF), (((0,), (0,)), ((), ())),
            preferred_element_type=F32,
        ).astype(BF)
        for g in range(ROWS)
    ]
    heads = [jnp.concatenate([heads[p], heads[pairs + p]], axis=0) for p in range(pairs)]
    m = pairs * COLS
    for step in range(count):
        arrivals[step].wait()
        xs = [x_s[step, :pairs].reshape(m, 128), x_s[step, pairs:].reshape(m, 128)]
        c = dot(jnp.concatenate(xs, axis=1), centre)
        kept = []
        for k in range(2):
            ck = c[:, 128 * k : 128 * k + 128]
            n = (ck * lax.rsqrt(jnp.mean(ck * ck, axis=1, keepdims=True) + EPS)).astype(BF)
            g = dot(n, w1_s[...])
            gate, up = g[:, :256], g[:, 256:]
            h = ((gate + gate * jnp.tanh(gate)) * up).astype(BF)
            u = dot(h, w2_s[...])
            y_s[step, k * pairs : (k + 1) * pairs] = (
                (xs[k].astype(F32) + u[:, :128]).astype(BF).reshape(pairs, COLS, 128)
            )
            c2 = ck + u[:, 128:]
            kept.append((c2 * lax.rsqrt(jnp.mean(c2 * c2, axis=1, keepdims=True) + EPS)).astype(BF))
            leaving[2 * step + k].start()
        cc = jnp.concatenate(kept, axis=1)
        acc = jnp.zeros((COLS, 128), F32)
        for p in range(pairs):
            acc = acc + dot(cc[p * COLS : (p + 1) * COLS], heads[p])
        b_s[:, step] = acc.T.astype(BF).reshape(NC, GROUP * ROWS, COLS)
        biases[step].start()
    for copy in (*leaving, *biases):
        copy.wait()


def pair_call(x, w1, w2, wb, prior, after, start, count):
    block = (count, ROWS, COLS, 128)
    more = [a for a in (prior, after) if a is not None]
    n = 4 + len(more)
    return call(
        lambda *refs: pair_kernel(*refs, start=start, count=count),
        [(x.shape, BF), ((NC, count, GROUP * ROWS, COLS), BF)],
        (x, w1, w2, wb, *more),
        name="pair", far=(0, *range(4, n + 2)), aliases={} if prior is None else {4: 0},
        scratch=[
            pltpu.VMEM(block, BF), pltpu.VMEM(block, BF), pltpu.VMEM((NC, count, GROUP * ROWS, COLS), BF),
            pltpu.VMEM((128, 512), BF), pltpu.VMEM((256, 256), BF),
            *(pltpu.SemaphoreType.DMA((i * count,)) for i in (1, 2, 1)),
        ],
        flops=count * 3 * 10**9,
    )


def attention_kernel(
    t0, t1, t2, t3, own_ref, other_ref, *refs
):
    *biases, msg_ref, back_ref, xk_s, o_s = refs
    col, core = lax.axis_index("col"), lax.axis_index("atom") % NK
    xk_s[:, pl.ds(core, 1)] = own_ref[...].reshape(NZ, 1, TOKS, C_S)
    xk_s[:, pl.ds(1 - core, 1)] = other_ref[...].reshape(NZ, 1, TOKS, C_S)
    xk = xk_s[...].reshape(COLS, C_S)
    wide = GROUP * TOKS
    packed = (t0, t1, t2, t3)
    t = jnp.concatenate([p[:wide, :] for p in packed], axis=0)
    scores = dot_nt(t, xk)
    groups = [(col + NC - s) % NC for s in range(NC)]
    scores = jnp.concatenate(
        [
            scores[s * wide : (s + 1) * wide]
            + jnp.concatenate(
                [b[pl.ds(groups[s], 1)].reshape(b.shape[1] * GROUP * ROWS, COLS) for b in biases], axis=0
            ).astype(F32)
            for s in range(NC)
        ],
        axis=0,
    )
    top = jnp.max(scores, axis=1, keepdims=True)
    p = jnp.exp(scores - top)
    total = jnp.sum(p, axis=1, keepdims=True)
    mixed = (dot(p.astype(BF), xk) / total).astype(BF)
    blocks = TOKS // ROWS
    lane_head = iota((1, GROUP, 1, GW), 3) // HEAD
    row_head = iota((1, GROUP, 1, GW), 1)
    lane16 = iota((1, GROUP, 1, 128), 3) % H_T
    row16 = iota((1, GROUP, 1, 128), 1)
    tops = jnp.zeros((TOKS, 128), F32)
    totals = jnp.zeros((TOKS, 128), F32)
    for s, w in enumerate(packed):
        lo = s * wide
        o = dot_nt(mixed[lo : lo + wide], w[wide : wide + GW, :]).reshape(blocks, GROUP, ROWS, GW)
        o = jnp.sum(jnp.where(lane_head == row_head, o, 0.0), axis=1).reshape(TOKS, GW)
        o_s[pl.ds(groups[s], 1)] = o.reshape(1, TOKS, GW)
        folded = jnp.concatenate([w[wide + GW :, i * C_A : (i + 1) * C_A] for i in range(GW // FOLD)], axis=0)
        back_ref.buffer[pl.ds(groups[s], 1)] = folded.reshape(1, GW, C_A)
        here = lane16 == row16 + groups[s] * GROUP
        for value, which in ((top, 0), (total, 1)):
            part = jnp.broadcast_to(value[lo : lo + wide], (wide, 128)).reshape(blocks, GROUP, ROWS, 128)
            part = jnp.sum(jnp.where(here, part, 0.0), axis=1).reshape(TOKS, 128)
            if which == 0:
                tops = tops + part
            else:
                totals = totals + part
    part_of = iota((TOKS, 128), 1) // H_T
    stats = jnp.zeros((TOKS, 128), F32)
    for i, piece in enumerate((*three(tops), *three(totals))):
        stats = jnp.where(part_of == i, piece.astype(F32), stats)
    msg_ref[...] = jnp.concatenate([o_s[g] for g in range(NC)] + [stats], axis=1).astype(BF)


def final_kernel(m0, m1, m2, m3, token_in_ref, state_ref, counts_ref, wback_ref, back_ref, out_ref):
    msgs = [m0[...], m1[...], m2[...], m3[...]]
    r, c = iota((128, 256), 0), iota((128, 256), 1)
    pick = ((r // H_T) // 3 == c // 128) & (r % H_T == c % H_T) & (r < 6 * H_T)
    stats = dot(jnp.concatenate([m[:, C_S:] for m in msgs], axis=0), jnp.where(pick, 1.0, 0.0).astype(BF))
    tops = [stats[i * TOKS : (i + 1) * TOKS, :128] for i in range(NC)]
    totals = [stats[i * TOKS : (i + 1) * TOKS, 128:] for i in range(NC)]
    top = jnp.maximum(jnp.maximum(tops[0], tops[1]), jnp.maximum(tops[2], tops[3]))
    shares = [l * jnp.exp(t - top) for l, t in zip(totals, tops)]
    whole = shares[0] + shares[1] + shares[2] + shares[3]
    r, c = iota((128, C_S), 0), iota((128, C_S), 1)
    expand = jnp.where((r % H_T == c // HEAD) & (r < 2 * H_T), 1.0, 0.0).astype(BF)
    part_of = iota((TOKS, 128), 1) // H_T
    coefs = []
    for share in shares:
        hi, lo = hi_lo(share / whole)
        coefs.append(jnp.where(part_of == 0, hi.astype(F32), lo.astype(F32)).astype(BF))
    scale = dot(jnp.concatenate(coefs, axis=0), expand)
    mix = jnp.zeros((TOKS, C_S), F32)
    for i, m in enumerate(msgs):
        mix = mix + scale[i * TOKS : (i + 1) * TOKS] * m[:, :C_S].astype(F32)
    folded = dot(mix.astype(BF), back_ref[...].reshape(C_S, C_A))
    returned = dot(token_in_ref[...].astype(BF), wback_ref[...]) + folded
    row, _, end_row, _ = spans(counts_ref)
    slots = iota((ATOMS, TOKS), 0).astype(F32)
    onehot = jnp.where((slots < end_row) & (slots >= end_row - row), 1.0, 0.0).astype(BF)
    r_hi, r_lo = hi_lo(returned)
    spread = dot(onehot, r_hi) + dot(onehot, r_lo)
    alive = iota((ATOMS, C_A), 0) < jnp.sum(counts_ref[...], axis=1, keepdims=True)
    out_ref[...] = jnp.where(alive, state_ref[...] + spread, 0.0).astype(BF)


def around(array, axis, size):
    return [lax.ppermute(array, axis, [(i, (i + s) % size) for i in range(size)]) for s in range(1, size)]


def local(
    atom_single, positions, noise_index, token_counts, token_single, pair_repr, w_pos, atom_wq, atom_wk, atom_wv,
    atom_wo, w_pool, trans_w1, trans_w2, w_bias, token_wq, token_wk, token_wv, token_wo, w_back,
):
    atoms = NY * NZ * NK
    counts = token_counts.reshape(1, TOKS)
    initial, normed, inner, outer = call(
        atom_in_kernel,
        [((ATOMS, C_A), F32), ((ATOMS, C_A), BF), ((MARGIN, 2 * C_A), BF), ((MARGIN, 2 * C_A), BF)],
        (noise_index, positions, w_pos, atom_single, counts),
        name="atom_in", smem=(0,), flops=10**8,
    )
    outer = lax.ppermute(outer, "atom", [(i, i + (1 if i % 2 else -1)) for i in range(1, atoms - 1)])
    inner = lax.ppermute(inner, "atom", [(i, i ^ 1) for i in range(atoms)])
    pair_out, biases = None, []

    def pair(i, after=None):
        nonlocal pair_out
        pair_out, bias = pair_call(pair_repr, trans_w1, trans_w2, w_bias.T, pair_out, after, *CHUNKS[i])
        biases.append(bias)

    pair(0)
    state, token_in, token_normed, t_own = call(
        atom_mid_kernel,
        [((ATOMS, C_A), F32), ((TOKS, C_S), F32), ((TOKS, C_S), BF), ((GROUP * TOKS + GW + FOLD, C_S), BF)],
        (
            normed, inner, outer, counts, atom_wq, atom_wk, atom_wv, initial, atom_wo, w_pool, token_single,
            token_wq.T, token_wk.T, token_wv.T, token_wo, w_back,
        ),
        name="atom_mid", flops=10**9,
    )
    flip = [
        ((y * NZ * NK + i) * NC + x, (x * NZ * NK + i) * NC + y)
        for y in range(NY) for i in range(NZ * NK) for x in range(NC)
    ]
    turned = lax.ppermute(token_normed, ("atom", "col"), flip)
    lines = [[(y * NZ + z) * NK + k for z in range(NZ)] for y in range(NY) for k in range(NK)]
    turned, biases[0], t_own = lax.optimization_barrier((turned, biases[0], t_own))
    own = lax.all_to_all(
        jnp.broadcast_to(turned[None], (NZ, TOKS, C_S)), "atom", 0, 0, axis_index_groups=lines, tiled=True
    )
    one = lax.ppermute(t_own, "col", [(i, (i + 1) % NC) for i in range(NC)])
    three_on = lax.ppermute(t_own, "col", [(i, (i - 1) % NC) for i in range(NC)])
    two = lax.ppermute(one, "col", [(i, (i + 1) % NC) for i in range(NC)])
    pair(1)
    packed = [t_own, one, two, three_on]
    own, biases[1] = lax.optimization_barrier((own, biases[1]))
    other = lax.ppermute(own, "atom", [(i, i ^ 1) for i in range(atoms)])
    for i in range(2, len(CHUNKS)):
        pair(i)

    msg, back = call(
        attention_kernel,
        [((TOKS, C_S + 128), BF), ((NC, GW, C_A), BF)],
        (*packed, own, other, *biases),
        name="attention", flops=3 * 10**9,
        scratch=[pltpu.VMEM((NZ, NK, TOKS, C_S), BF), pltpu.VMEM((NC, TOKS, GW), F32)],
    )
    msgs = [msg] + around(msg, "col", NC)
    (atom_out,) = call(
        final_kernel, [((ATOMS, C_A), BF)], (*msgs, token_in, state, counts, w_back, back),
        name="final", flops=10**8,
    )
    return (atom_out, pair_out)


def solution(mesh):
    placed = (
        P("atom", None), P(None, "atom"), P(), P("atom"), P("atom", None), P("atom", "col", None),
        P(), P(), P(), P(), P(), P(), P(), P(), P(),
        P(None, "col"), P(None, "col"), P(None, "col"), P("col", None), P(),
    )
    return jax.shard_map(
        local,
        mesh=mesh,
        in_specs=placed,
        out_specs=(P("atom", None), P("atom", "col", None)),
        check_vma=False,
    )
```
